32 devices in a mesh: cube: 8 (over z, y), front: 4 (over x, core).
Axes of the slice: x: 2, y: 2, z: 4, core: 2. Of those that a mesh axis runs over, the one named last changes fastest.
Arguments:
- kkt_blocks: float32 [4, 2048, 128], P('front', 'cube'), may hold values from -1.5 to 1.5
- kkt_owner: int32 [4, 2048, 1], P('front', 'cube'), may hold values from 0 to 7; in each aligned block of 256 rows (0 to 255, 256 to 511, ..., all dimensions but the last counted through in order) at most 64 rows name the same one
- kkt_target: int32 [4, 2048], P('front', 'cube'), may hold values from 0 to 255
- leaf_pivot: float32 [16, 512, 128], P('cube', 'front'), may hold values from -3.5 to 3.5
- pivot_signs: int32 [16, 512], P('cube', 'front'), may hold values from -1 to 1, as said below
- perturb: float32 [16, 512], P('cube', 'front'), may hold values from 0.25 to 1
- leaf_coupling: float32 [16, 512, 128], P('cube', 'front'), may hold values from -1.5 to 1.5
- leaf_map: int32 [16, 512], P('cube', 'front'), may hold values from 256 to 2047
- mid_front: bfloat16 [8192, 2048], P('cube', 'front'), may hold values from -3.5 to 3.5
- level_map: int32 [4, 2048], replicated, may hold values from 256 to 2047, as said below
- top_front: bfloat16 [4096, 2048], P('cube', 'front'), may hold values from -3.5 to 3.5
Outputs:
- leaf_factor: float32 [16, 512, 128], P('cube', 'front')
- mid_factor: float32 [8192, 256], P(('cube', 'front'))
- upper_schur: float32 [4096, 2048], P('cube', 'front')
The draws below stay inside these ranges and needn't reach their ends.
Inputs may be any that keep to these rules, and one draw needn't show every extreme that they name: `kkt_owner`: the rows of one device name one cube index at most 64 times, and some cube index exactly 64 times. `pivot_signs`: every entry is -1 or 1. `level_map`: position p of a level-1 front goes to a position of the same quarter floor(p / 512) of the level-2 front, never below 256.
All inputs are finite; a program needn't handle non-finite values.
Results may differ from the reference program's by a relative error of at most 0.0003.
Values sent between devices are 32-bit elements; how exact they have to be, the bound alone decides.
No kernel may reach another device: no remote copies, remote signals or barrier semaphores. Data moves between devices by JAX's collectives and lax.ppermute only.
A program may use at most 64 MiB of HBM per device.

```python
import math
import jax
import jax.numpy as jnp
import numpy as np
from jax import lax

NU = 2048
PIV = 128
RL = 128
PANELS = 2
NS_STEPS = 2
NF = 2
NB = 256
KU = 256
CAP = 64
N_CUBE = 8
N_FRONT = 4


def sign_table(key):
    return 2 * jax.random.randint(jax.random.fold_in(key, 11), (N_CUBE * NF, N_FRONT * PIV), 0, 2) - 1


def draw_pivot_signs(key, part):
    return sign_table(key).astype(jnp.int32)


def draw_leaf_pivot(key, part):
    sign_part = sign_table(key).astype(jnp.float32).reshape(N_CUBE * NF, N_FRONT, PIV)
    key_one, key_two = jax.random.split(jax.random.fold_in(key, 12))
    spread = jax.random.uniform(key_one, sign_part.shape, jnp.float32)
    magnitude = 1.5 + 2.0 * spread
    noise_part = jax.random.uniform(key_two, (N_CUBE * NF, N_FRONT, PIV, PIV), jnp.float32, -1.0, 1.0)
    noise_part = (noise_part + jnp.swapaxes(noise_part, -1, -2)) * (0.25 / math.sqrt(PIV))
    identity = jnp.eye(PIV, dtype=jnp.float32)
    matrix = noise_part * (1.0 - identity) + identity * (sign_part * magnitude)[..., None, :]
    return matrix.reshape(N_CUBE * NF, N_FRONT * PIV, PIV)


def front_entries(key, positions, salt):
    row_count = positions.shape[0]
    key_list = jax.random.split(jax.random.fold_in(key, salt), 4)
    base_part = jnp.clip(jax.random.normal(key_list[0], (row_count, NU), jnp.float32), -4.0, 4.0) * 0.3
    small_part = jax.random.uniform(key_list[1], (row_count, NU), jnp.float32, -1.0, 1.0) * (0.35 / math.sqrt(PIV))
    magnitude = jax.random.uniform(key_list[2], (row_count,), jnp.float32, 1.5, 3.5)
    sign_part = (2 * jax.random.randint(key_list[3], (row_count,), 0, 2) - 1).astype(jnp.float32)
    columns = jnp.arange(NU)
    pivot_area = (positions[:, None] < PANELS * PIV) & (columns[None, :] < PANELS * PIV)
    diagonal = positions[:, None] == columns[None, :]
    values = jnp.where(pivot_area, small_part, base_part)
    values = jnp.where(diagonal & pivot_area, (sign_part * magnitude)[:, None], values)
    return values


def draw_mid_front(key, part):
    positions = jnp.arange(N_CUBE * (NU // 2)) % NU
    return front_entries(key, positions, 21).astype(jnp.bfloat16)


def draw_top_front(key, part):
    all_rows = jnp.arange(N_CUBE * (NU // 4))
    device = all_rows // (NU // 4)
    inner_row = all_rows % (NU // 4)
    row_quarter = 2 * (device % 2) + device // 2 % 2
    positions = row_quarter * (NU // 4) + inner_row
    return front_entries(key, positions, 22).astype(jnp.bfloat16)


def draw_level_map(key, part):
    columns = jnp.broadcast_to(jnp.arange(NU, dtype=jnp.int32), (N_CUBE // 2, NU))
    quarter = columns // (NU // 4)
    lowest = jnp.where(quarter == 0, PANELS * PIV, 0).astype(jnp.int32)
    offset = jax.random.randint(jax.random.fold_in(key, 31), (N_CUBE // 2, NU), lowest, NU // 4)
    return (quarter * (NU // 4) + offset).astype(jnp.int32)


def touch_ends(drawn, own_key, low, largest):
    longest = drawn.shape.index(max(drawn.shape))
    spots = []
    for shift in (0, 1):
        where = [jax.random.randint(jax.random.fold_in(own_key, axis), (), 0, length) for axis, length in enumerate(drawn.shape)]
        where[longest] = (where[longest] + shift) % drawn.shape[longest]
        spots.append(tuple(where))
    return drawn.at[spots[0]].set(low).at[spots[1]].set(largest)


def block_levels(rng, shape, pieces, least, top_value):
    def one(position, parts):
        steps = jax.random.uniform(jax.random.fold_in(jax.random.fold_in(rng, 6), position), (parts,), jnp.float32, least / len(pieces), top_value / len(pieces))
        return jnp.repeat(jnp.exp(steps), shape[position] // parts).reshape((-1,) + (1,) * (len(shape) - position - 1))

    level = one(*pieces[0])
    for cut in pieces[1:]:
        level = level * one(*cut)
    return level


def assign_block(rng, own, number, rows, count, top, limit, skew):
    ranking = jax.random.permutation(rng, count)
    packed, ordinary = portions_of(count, rows * top, limit, skew, True), portions_of(count, rows * top, limit, skew, False)
    places = jnp.arange(count)

    def named(sizes, offset_by):
        used = int((sizes > 0).sum())
        fixed = max(1, used // 4)
        passed = fixed + (places - fixed + offset_by * (used - fixed)) % max(1, count - fixed)
        return jnp.zeros((count,), jnp.int32).at[ranking[jnp.where(places < fixed, places, passed)]].set(jnp.asarray(sizes, jnp.int32))

    sizes = jnp.where(number % 4 == 0, named(packed, number // 4), named(ordinary, number - number // 4 - 1))
    mixed = jax.random.permutation(jax.random.fold_in(own, 3), count)
    giver, taker = mixed[0:count // 2 * 2:2], mixed[1:count // 2 * 2:2]
    slack = jnp.minimum(sizes[giver] - 1, limit - sizes[taker]) // 2
    slack = jnp.where((giver == ranking[0]) | (taker == ranking[0]) | (sizes[taker] == 0), 0, jnp.maximum(slack, 0))
    passed = jax.random.randint(jax.random.fold_in(own, 4), (count // 2,), 0, 1 << 20) % (slack + 1)
    sizes = sizes.at[giver].add(-passed).at[taker].add(passed)
    labels = jnp.searchsorted(jnp.cumsum(sizes), jnp.arange(rows * top), side="right").astype(jnp.int32)
    grid = labels.reshape(top, rows).T
    grid = grid[jax.random.permutation(jax.random.fold_in(own, 1), rows)]
    offset_by = jax.random.randint(jax.random.fold_in(own, 2), (rows, 1), 0, top)
    return jnp.take_along_axis(grid, (jnp.arange(top)[None, :] + offset_by) % top, axis=1)


def portions_of(number_of, total, bound, slope, full):
    weights = [(1 << 20) // math.isqrt(standing ** slope) + 1 for standing in range(1, number_of + 1)]
    largest = bound if full else min(bound, max(-(-total // number_of), total * weights[0] // sum(weights)))
    least = 1 if total - largest >= number_of - 1 else 0
    holding, surplus = [largest] + [least] * (number_of - 1), total - largest - least * (number_of - 1)
    while surplus > 0:
        free = [i for i in range(1, number_of) if holding[i] < largest] or [i for i in range(1, number_of) if holding[i] < bound]
        pool, left = sum([weights[i] for i in free]), surplus
        for i in free:
            more = min(bound - holding[i], max(1, left * weights[i] // pool), surplus)
            holding[i] = holding[i] + more
            surplus = surplus - more
    return np.array(holding)


def bell_draw(key, dims, deviation, limit, cuts=(), kind=jnp.bfloat16):
    entries = deviation * jax.random.normal(key, dims, jnp.float32)
    if cuts:
        entries = entries * block_levels(key, dims, cuts, -0.22, 0.18)
    return jnp.clip(entries, -limit, limit).astype(kind)


def setup_inputs(seed: int = 0) -> dict:
    splits = jax.random.split(jax.random.key(seed), 12)
    kkt_blocks = bell_draw(splits[0], (N_FRONT, N_CUBE * NB, PIV), 0.25, 1.5, ((0, 4), (1, 8)), jnp.float32)
    kkt_owner_keys = jax.random.split(jax.random.fold_in(splits[1], 1), N_FRONT * (N_CUBE * NB) // NB)
    kkt_owner_turns = jax.random.permutation(jax.random.fold_in(splits[1], 3), N_FRONT * (N_CUBE * NB) // NB)
    kkt_owner = jax.vmap(lambda own, number: assign_block(jax.random.fold_in(splits[1], 2), own, number, NB, N_CUBE, 1, CAP, 2))(kkt_owner_keys, kkt_owner_turns).reshape((N_FRONT, N_CUBE * NB, 1))
    kkt_target = touch_ends(jax.random.randint(splits[2], (N_FRONT, N_CUBE * NB), 0, NF * RL), jax.random.fold_in(splits[2], 1), 0, (NF * RL) - 1).astype(jnp.int32)
    leaf_pivot = draw_leaf_pivot(jax.random.fold_in(splits[11], 71), 0)
    pivot_signs = draw_pivot_signs(jax.random.fold_in(splits[11], 71), 0)
    perturb = jnp.clip(jnp.exp(math.log(1.0) - 1.3862944 * jax.random.uniform(splits[5], (N_CUBE * NF, N_FRONT * PIV), jnp.float32) ** block_levels(splits[5], (N_CUBE * NF, N_FRONT * PIV), ((0, 8), (1, 4)), -0.2, 0.2)), 0.25, 1.0)
    leaf_coupling = bell_draw(splits[6], (N_CUBE * NF, N_FRONT * RL, PIV), 0.25, 1.5, ((0, 8), (1, 4)), jnp.float32)
    leaf_map = touch_ends(jax.random.randint(splits[7], (N_CUBE * NF, N_FRONT * RL), KU, NU), jax.random.fold_in(splits[7], 1), KU, NU - 1).astype(jnp.int32)
    mid_front = draw_mid_front(jax.random.fold_in(splits[11], 71), 0)
    level_map = draw_level_map(jax.random.fold_in(splits[11], 71), 0)
    top_front = draw_top_front(jax.random.fold_in(splits[11], 71), 0)
    return {"kkt_blocks": kkt_blocks, "kkt_owner": kkt_owner, "kkt_target": kkt_target, "leaf_pivot": leaf_pivot, "pivot_signs": pivot_signs, "perturb": perturb, "leaf_coupling": leaf_coupling, "leaf_map": leaf_map, "mid_front": mid_front, "level_map": level_map, "top_front": top_front}


HIGHEST = lax.Precision.HIGHEST


def newton_inverse(pivot_block):
    diagonal = jnp.diagonal(pivot_block, axis1=-2, axis2=-1)
    current = jnp.eye(pivot_block.shape[-1], dtype=jnp.float32) * (1.0 / diagonal)[..., None, :]
    for sweep_index in range(NS_STEPS):
        product = jnp.einsum("...ij,...jk->...ik", pivot_block, current, precision=HIGHEST)
        current = 2.0 * current - jnp.einsum("...ij,...jk->...ik", current, product, precision=HIGHEST)
    return current


def eliminate(front_matrix):
    positions = jnp.arange(NU)
    factors = []
    for panel_index in range(PANELS):
        first_col = panel_index * PIV
        finish = first_col + PIV
        columns = front_matrix[:, first_col:finish]
        inverse = newton_inverse(columns[first_col:finish])
        keep_rows = (positions >= finish).astype(jnp.float32)[:, None]
        lower_rows = jnp.dot(columns, inverse, precision=HIGHEST) * keep_rows
        front_matrix = front_matrix - jnp.dot(lower_rows, (columns * keep_rows).T, precision=HIGHEST)
        factors.append(lower_rows)
    return front_matrix, jnp.concatenate(factors, axis=1)


def one_group(inputs):
    leaf_terms, leaf_maps, mid_parts, level_links, top_part = inputs
    positions = jnp.arange(NU)
    kept_rows = positions >= PANELS * PIV
    link_terms = []
    link_ids = []
    factors = []
    for child_index in range(2):
        mapping = leaf_maps[child_index]
        flat_index = mapping[..., :, None] * NU + mapping[..., None, :]
        assembled = jax.ops.segment_sum(leaf_terms[child_index].reshape(-1), flat_index.reshape(-1), num_segments=NU * NU)
        schur_part, lower_rows = eliminate(mid_parts[child_index].astype(jnp.float32) + assembled.reshape(NU, NU))
        factors.append(lower_rows)
        links = level_links[child_index]
        pair_ids = jnp.where(kept_rows[:, None] & kept_rows[None, :], links[:, None] * NU + links[None, :], NU * NU)
        link_ids.append(pair_ids.reshape(-1))
        link_terms.append(schur_part.reshape(-1))
    top_added = jax.ops.segment_sum(jnp.concatenate(link_terms), jnp.concatenate(link_ids), num_segments=NU * NU + 1)[:-1]
    final_front, unused = eliminate(top_part.astype(jnp.float32) + top_added.reshape(NU, NU))
    return final_front, jnp.stack(factors)


def reference(kkt_blocks, kkt_owner, kkt_target, leaf_pivot, pivot_signs, perturb, leaf_coupling, leaf_map, mid_front, level_map, top_front):
    owner_index = kkt_owner[:, :, 0]
    front_index = jnp.arange(N_FRONT, dtype=jnp.int32)[:, None]
    flat_rows = (owner_index * NF + kkt_target // RL) * (N_FRONT * RL) + front_index * RL + kkt_target % RL
    arrivals = jax.ops.segment_sum(kkt_blocks.reshape(-1, PIV), flat_rows.reshape(-1), num_segments=N_CUBE * NF * N_FRONT * RL)
    coupling = (leaf_coupling + arrivals.reshape(N_CUBE * NF, N_FRONT * RL, PIV)).reshape(N_CUBE * NF, N_FRONT, RL, PIV)
    identity = jnp.eye(PIV, dtype=jnp.float32)
    shifts = (pivot_signs.astype(jnp.float32) * perturb).reshape(N_CUBE * NF, N_FRONT, PIV)
    pivots = leaf_pivot.reshape(N_CUBE * NF, N_FRONT, PIV, PIV) + identity * shifts[..., None, :]
    inverse = newton_inverse(pivots)
    factor = jnp.einsum("lfrk,lfkj->lfrj", coupling, inverse, precision=HIGHEST)
    contrib = -jnp.einsum("lfrk,lfsk->lfrs", factor, coupling, precision=HIGHEST)
    groups = N_CUBE // 4
    leaf_terms = contrib.reshape(groups, 2, 2, NF, N_FRONT, RL, RL)
    leaf_maps = leaf_map.reshape(groups, 2, 2, NF, N_FRONT, RL)
    mid_parts = mid_front.reshape(groups, 2, NU, NU)
    level_links = level_map.reshape(groups, 2, NU)
    top_parts = jnp.transpose(top_front.reshape(groups, 2, 2, NU // 4, NU), (0, 2, 1, 3, 4)).reshape(groups, NU, NU)
    finals, mid_factors = lax.map(one_group, (leaf_terms, leaf_maps, mid_parts, level_links, top_parts))
    upper_schur = jnp.transpose(finals.reshape(groups, 2, 2, NU // 4, NU), (0, 2, 1, 3, 4)).reshape(N_CUBE * NU // 4, NU)
    mid_factor = mid_factors.reshape(N_CUBE * NU // 2, PANELS * PIV)
    leaf_factor = factor.reshape(N_CUBE * NF, N_FRONT * RL, PIV)
    return leaf_factor, mid_factor, upper_schur
```

```python
import functools

import jax
import jax.numpy as jnp
from jax import lax
from jax.experimental import pallas as pl
from jax.experimental.pallas import tpu as pltpu
from jax.sharding import PartitionSpec as P

NU = 2048
PIV = 128
KU = 256
QUARTER = NU // 4
HALF = NU // 2

HIGHEST = lax.Precision.HIGHEST
F32 = jnp.float32
BF16 = jnp.bfloat16
AXES = ("cube", "front")
NN = (((1,), (0,)), ((), ()))
NT = (((1,), (1,)), ((), ()))


def mm(a, b, dims=NN):
    return lax.dot_general(a, b, dims, preferred_element_type=F32)


def exact(a, b, dims=NN):
    return lax.dot_general(a, b, dims, preferred_element_type=F32, precision=HIGHEST)


def split(x):
    high = x.astype(BF16)
    return high, (x - high.astype(F32)).astype(BF16)


def split3(x):
    high = x.astype(BF16)
    rest = x - high.astype(F32)
    mid = rest.astype(BF16)
    return high, mid, (rest - mid.astype(F32)).astype(BF16)


def mm3(a, b, dims=NN):
    ah, al = split(a)
    bh, bl = split(b)
    return mm(ah, bh, dims) + (mm(ah, bl, dims) + mm(al, bh, dims))


def iota(shape, axis):
    return lax.broadcasted_iota(jnp.int32, shape, axis)


def onehot(mask):
    return jnp.where(mask, 1.0, 0.0).astype(BF16)


def newton_inverse(block):
    size = block.shape[0]
    eye = iota((size, size), 0) == iota((size, size), 1)
    diagonal = jnp.where(eye, block, 0.0)
    row = 1.0 / jnp.sum(diagonal, axis=0, keepdims=True)
    col = 1.0 / jnp.sum(diagonal, axis=1, keepdims=True)
    current = jnp.where(eye, 2.0 * row, 0.0) - col * (block * row)
    return 2.0 * current - exact(current, exact(block, current))


def pack_kernel(capacity, slots, cube_count, blocks, owner, target, out):
    count = blocks.shape[0]
    owners = owner[...]
    named = iota((max(cube_count, 16), count), 0) == owners
    earlier = onehot(iota((count, count), 0) < iota((count, count), 1))
    ranks = mm(onehot(named), earlier)
    rank = jnp.sum(jnp.where(named, ranks, 0.0), axis=0, keepdims=True).astype(jnp.int32)
    first = owners * slots
    spots = iota((cube_count * slots, count), 0)
    place = onehot(spots == first + rank)
    high, mid, low = split3(blocks[...])
    values = mm(place, high) + (mm(place, mid) + mm(place, low))
    tags = jnp.where(spots == first + capacity, target[...].astype(F32), 0.0).astype(BF16)
    lanes = onehot(iota((blocks.shape[1], count), 0) == rank)
    out[...] = values + mm(tags, lanes, NT)


def prepare_kernel(where, leaf_pivot, signs, perturb, leaf_map, level_map, inverse, links):
    size = leaf_pivot.shape[1]
    eye = iota((size, size), 0) == iota((size, size), 1)
    table = level_map[pl.ds(where[4], 1), :]
    rows = iota((16, NU), 0)
    digits = jnp.where(rows == 0, table // 256, jnp.where(rows == 1, table % 256, 0))
    digits = digits.astype(F32).astype(BF16)
    links[...] = jnp.zeros(links.shape, F32)
    for leaf in range(leaf_pivot.shape[0]):
        shift = signs[leaf : leaf + 1, :].astype(F32) * perturb[leaf : leaf + 1, :]
        inverse[leaf] = newton_inverse(leaf_pivot[leaf] + jnp.where(eye, shift, 0.0))
        found = mm(digits, onehot(iota((NU, size), 0) == leaf_map[leaf : leaf + 1, :]))
        links[leaf : leaf + 1, :] = found[0:1, :] * 256.0 + found[1:2, :]


def leaf_kernel(capacity, slots, cube_count, got, inverse, links, coupling, factor, sent):
    leaves, rows, width = coupling.shape

    def arrivals(cube):
        block = got[cube]
        tags = block[capacity : capacity + 1, :].astype(jnp.int32)
        here = (iota((leaves * rows, width), 0) == tags) & (iota((leaves * rows, width), 1) < capacity)
        values = block
        if slots < width:
            values = jnp.concatenate([block, jnp.zeros((width - slots, width), F32)], axis=0)
        return onehot(here), values

    if cube_count <= 16:
        pairs = [arrivals(cube) for cube in range(cube_count)]
        place = jnp.concatenate([here for here, _ in pairs], axis=1)
        high, mid, low = split3(jnp.concatenate([values for _, values in pairs], axis=0))
        added = mm(place, high) + (mm(place, mid) + mm(place, low))
    else:

        def step(cube, total):
            here, values = arrivals(cube)
            high, mid, low = split3(values)
            return total + (mm(here, high) + (mm(here, mid) + mm(here, low)))

        added = lax.fori_loop(0, cube_count, step, jnp.zeros((leaves * rows, width), F32))
    for leaf in range(leaves):
        rhs = coupling[leaf] + added[leaf * rows : (leaf + 1) * rows, :]
        part = exact(rhs, inverse[leaf])
        factor[leaf] = part
        sent[leaf, 0:rows, :] = -mm3(part, rhs, NT)
        sent[leaf, rows : rows + 8, :] = jnp.where(
            iota((8, width), 0) == 0, links[leaf : leaf + 1, :], 0.0
        )


def panel_parts(pivots):
    upper = newton_inverse(pivots[0:PIV, 0:PIV])
    below = pivots[PIV:KU, 0:PIV]
    lower = newton_inverse(
        pivots[PIV:KU, PIV:KU] - exact(exact(below, upper), below, NT)
    )
    return upper, below, lower


def panel_rows(rows, first, upper, below, lower):
    position = first + iota((rows.shape[0], PIV), 0)
    left = jnp.where(position >= PIV, mm3(rows[:, 0:PIV], upper), 0.0)
    right = rows[:, PIV:KU] - mm3(left, below, NT)
    last = jnp.where(position >= KU, mm3(right, lower), 0.0)
    keep = jnp.concatenate(
        [jnp.where(position >= PIV, rows[:, 0:PIV], 0.0), jnp.where(position >= KU, right, 0.0)], axis=1
    )
    return jnp.concatenate([left, last], axis=1), keep


def mid_kernel(where, front, from_x, from_y, from_core, pair, far, factor, left, cols, send, rows):
    low, high, pos = where[0], where[1], where[2]
    is_low = low == 0

    @pl.when(pos == 0)
    def _():
        rows[...] = front[:, 0:KU].astype(F32)

    @pl.when(pos == 2)
    def _():
        rows[...] = from_x[...]

    @pl.when(pos % 2 == 1)
    def _():
        rows[...] = from_core[0:HALF, :]

    own_cols = pl.multiple_of((pos % 2) * QUARTER, QUARTER)
    held = (pos // 2) == low
    other_cols = jnp.where(
        pos == 0,
        from_y[0:QUARTER, :],
        jnp.where(
            pos == 1, from_core[HALF : HALF + QUARTER, :], jnp.where(pos == 2, pair[...], far[...])
        ),
    )
    col_rows = jnp.where(held, rows[pl.ds(own_cols, QUARTER), :], other_cols)
    other_pivots = jnp.where(pos == 1, from_core[HALF + QUARTER :, :], other_cols[0:KU, :])
    pivots = jnp.where(is_low, rows[0:KU, :], other_pivots)
    upper, below, lower = panel_parts(pivots)
    row_left, _ = panel_rows(rows[...], low * HALF, upper, below, lower)
    _, col_keep = panel_rows(col_rows, pos * QUARTER, upper, below, lower)
    left[...] = row_left
    cols[...] = col_keep
    slab = HALF // 4
    factor[...] = left[pl.ds(pl.multiple_of(pos * slab, slab), slab), :]
    start = pl.multiple_of((1 - high) * QUARTER, QUARTER)
    send[...] = front[pl.ds(start, QUARTER), :].astype(F32) - mm3(
        left[pl.ds(start, QUARTER), :], col_keep, NT
    )


def spread(values, level_map, group, row_quarter, col_quarter):
    def places(quarter):
        start = pl.multiple_of(quarter * QUARTER, QUARTER)
        target = level_map[pl.ds(group, 1), pl.ds(start, QUARTER)] - start
        from_pos = start + iota((1, QUARTER), 1)
        target = jnp.where(from_pos >= KU, target, -1)
        return onehot(iota((QUARTER, QUARTER), 0) == target)

    row_place = places(row_quarter)
    col_place = places(col_quarter)
    high, low = split(values)
    high, low = split(mm(row_place, high) + mm(row_place, low))
    return mm(high, col_place, NT) + mm(low, col_place, NT)


def own_kernel(where, front, left, cols, level_map, base, out):
    start = pl.multiple_of(where[1] * QUARTER, QUARTER)
    block = front[pl.ds(start, QUARTER), :].astype(F32) - mm3(
        left[pl.ds(start, QUARTER), :], cols[...], NT
    )
    out[...] = base[...] + spread(block, level_map, where[4], where[3], where[2])


def other_kernel(where, block, level_map, base, out):
    group = where[4] + 1 - 2 * where[1]
    out[...] = base[...] + spread(block[...], level_map, group, where[3], where[2])


def top_kernel(where, front, from_x, from_core, from_y, from_z, pivots_z, out, rows):
    low, high, pos, quarter = where[0], where[1], where[2], where[3]

    @pl.when(pos == 0)
    def _():
        rows[...] = front[:, 0:KU].astype(F32)

    @pl.when(pos == 2)
    def _():
        rows[...] = from_x[...]

    @pl.when(pos % 2 == 1)
    def _():
        rows[...] = from_core[...]

    own = rows[...]
    col_rows = jnp.where(
        quarter == pos, own, jnp.where(high == pos % 2, from_y[...], from_z[...])
    )
    pivots = jnp.where(
        pos == 0,
        col_rows[0:KU, :],
        jnp.where(
            high == 1, pivots_z[...], jnp.where(low == 0, own[0:KU, :], from_y[0:KU, :])
        ),
    )
    upper, below, lower = panel_parts(pivots)
    row_left, _ = panel_rows(own, quarter * QUARTER, upper, below, lower)
    _, col_keep = panel_rows(col_rows, pos * QUARTER, upper, below, lower)
    out[...] = front[...].astype(F32) - mm3(row_left, col_keep, NT)


def gather_kernel(count, where, *refs):
    own, swapped, base, out = refs[0:count], refs[count], refs[count + 1], refs[count + 2]
    row_first = where[3] * QUARTER
    col_first = where[2] * QUARTER
    width = own[0].shape[2]
    leaves = own[0].shape[0]
    total = base[...]
    for chip in range(count):
        places, highs, lows = [], [], []
        for source in (own[chip], swapped.at[chip]):
            for leaf in range(leaves):
                link = source[leaf, width : width + 1, :].astype(jnp.int32)
                spots = iota((QUARTER, width), 0)
                places.append(onehot(spots == link - row_first))
                cols = onehot(spots == link - col_first)
                high, low = split(source[leaf, 0:width, :])
                high, low = split(mm(high, cols, NT) + mm(low, cols, NT))
                highs.append(high)
                lows.append(low)
        place = jnp.concatenate(places, axis=1)
        total = total + (
            mm(place, jnp.concatenate(highs, axis=0)) + mm(place, jnp.concatenate(lows, axis=0))
        )
    out[...] = total


def call(body, outs, args, scalars=True, scratch=(), flops=10**8):
    specs = [pl.BlockSpec(memory_space=pltpu.VMEM) for _ in args]
    if scalars:
        specs[0] = pl.BlockSpec(memory_space=pltpu.SMEM)
    shapes = [jax.ShapeDtypeStruct(shape, F32) for shape in outs]
    moved = sum(4 * functools.reduce(lambda a, b: a * b, shape) for shape in outs)
    single = len(shapes) == 1
    return pl.pallas_call(
        body,
        out_shape=shapes[0] if single else shapes,
        in_specs=specs,
        out_specs=(
            pl.BlockSpec(memory_space=pltpu.VMEM)
            if single
            else [pl.BlockSpec(memory_space=pltpu.VMEM) for _ in shapes]
        ),
        scratch_shapes=list(scratch),
        compiler_params=pltpu.CompilerParams(vmem_limit_bytes=40 * 2**20),
        cost_estimate=pl.CostEstimate(flops=flops, bytes_accessed=2 * moved, transcendentals=0),
    )(*args)


def local(
    kkt_blocks,
    kkt_owner,
    kkt_target,
    leaf_pivot,
    pivot_signs,
    perturb,
    leaf_coupling,
    leaf_map,
    mid_front,
    level_map,
    top_front,
):
    cube_count = lax.axis_size("cube")
    front_count = lax.axis_size("front")
    cube = lax.axis_index("cube")
    front = lax.axis_index("front")
    b0 = cube % 2
    b1 = cube // 2 % 2
    quarter = 2 * b0 + b1
    where = jnp.stack([b0, b1, front, quarter, cube // 2]).astype(jnp.int32)

    def move(array, rule):
        pairs = []
        for source_cube in range(cube_count):
            for source_front in range(front_count):
                target = rule(source_cube % 2, source_cube // 2 % 2, source_front)
                if target is not None:
                    new_cube = source_cube // 4 * 4 + 2 * target[1] + target[0]
                    pairs.append(
                        (source_cube * front_count + source_front, new_cube * front_count + target[2])
                    )
        return lax.ppermute(array, AXES, pairs)

    blocks = kkt_blocks[0]
    block_count, width = blocks.shape
    capacity = max(2, 2 * block_count // cube_count)
    slots = -(-(capacity + 1) // 8) * 8

    mid_cols = mid_front[:, 0:KU].astype(F32)
    top_cols = top_front[:, 0:KU].astype(F32)

    packed = call(
        functools.partial(pack_kernel, capacity, slots, cube_count),
        [(cube_count * slots, width)],
        [blocks, kkt_owner.reshape(1, block_count), kkt_target.reshape(1, block_count)],
        scalars=False,
    )
    got = lax.all_to_all(
        packed.reshape(cube_count, slots, width), "cube", split_axis=0, concat_axis=0, tiled=True
    )

    mid_x = move(mid_cols, lambda y, z, f: (y, z, 2) if f == 0 else None)
    mid_y = move(mid_cols, lambda y, z, f: (1 - y, z, 0) if f == 0 else None)
    mid_core = move(
        jnp.concatenate(
            [jnp.where(front == 0, mid_cols, mid_x), mid_y[QUARTER:HALF], mid_y[0:KU]], axis=0
        ),
        lambda y, z, f: (y, z, f + 1) if f % 2 == 0 else None,
    )
    mid_pair = move(mid_x[0:QUARTER], lambda y, z, f: (1 - y, z, 2) if f == 2 else None)
    mid_far = move(
        jnp.where(b0 == 0, mid_y[QUARTER:HALF], mid_y[0:QUARTER]),
        lambda y, z, f: (y, z, 3) if f == 0 else None,
    )

    top_x = move(top_cols, lambda y, z, f: (y, z, 2) if f == 0 else None)
    top_core = move(
        jnp.where(front == 0, top_cols, top_x), lambda y, z, f: (y, z, f + 1) if f % 2 == 0 else None
    )
    top_rows = jnp.where(front == 0, top_cols, jnp.where(front == 2, top_x, top_core))

    def down_y(y, z, f):
        if y == 0:
            return (1, z, f) if z == 0 or f == 1 else None
        return (0, z, f) if (z, f) in ((0, 2), (1, 3)) else None

    top_y = move(top_rows, down_y)
    top_z = move(
        jnp.where(quarter == front, top_rows, top_y),
        lambda y, z, f: (y, 1 - z, f) if z == f % 2 else None,
    )
    top_pivots = move(
        jnp.where(b0 == 0, top_rows[0:KU], top_y[0:KU]),
        lambda y, z, f: (y, 1, f) if z == 0 and f > 0 else None,
    )

    leaves = leaf_pivot.shape[0]
    size = leaf_pivot.shape[2]
    inverse, links = call(
        prepare_kernel,
        [(leaves, size, size), (8, size)],
        [where, leaf_pivot, pivot_signs, perturb, leaf_map, level_map],
    )
    factor, sent = call(
        functools.partial(leaf_kernel, capacity, slots, cube_count),
        [leaf_coupling.shape, (leaves, size + 8, size)],
        [got, inverse, links, leaf_coupling],
        scalars=False,
    )

    k_x = move(sent, lambda y, z, f: (y, z, f ^ 2))
    k_y = move(sent, lambda y, z, f: (1 - y, z, f))
    k_z = move(sent, lambda y, z, f: (y, 1 - z, f))
    k_xy = move(k_y, lambda y, z, f: (y, z, f ^ 2))
    k_yz = move(k_z, lambda y, z, f: (1 - y, z, f))
    k_xz = move(k_x, lambda y, z, f: (y, 1 - z, f))
    k_xyz = move(k_yz, lambda y, z, f: (y, z, f ^ 2))
    chips = [sent, k_x, k_y, k_z, k_xy, k_yz, k_xz, k_xyz]
    swapped = move(jnp.stack(chips), lambda y, z, f: (y, z, f ^ 1))

    mid_factor, mid_left, mid_keep, mid_send = call(
        mid_kernel,
        [(HALF // front_count, KU), (HALF, KU), (QUARTER, KU), (QUARTER, QUARTER)],
        [where, mid_front, mid_x, mid_y, mid_core, mid_pair, mid_far],
        scratch=[pltpu.VMEM((HALF, KU), F32)],
    )
    mid_other = move(mid_send, lambda y, z, f: (y, 1 - z, f))

    square = [(QUARTER, QUARTER)]
    upper = call(
        top_kernel,
        square,
        [where, top_front, top_x, top_core, top_y, top_z, top_pivots],
        scratch=[pltpu.VMEM((QUARTER, KU), F32)],
    )
    upper = call(own_kernel, square, [where, mid_front, mid_left, mid_keep, level_map, upper])
    upper = call(
        functools.partial(gather_kernel, len(chips)), square, [where, *chips, swapped, upper]
    )
    upper = call(other_kernel, square, [where, mid_other, level_map, upper])
    return factor, mid_factor, upper


def solution(mesh):
    in_specs = (
        P("front", "cube", None),
        P("front", "cube", None),
        P("front", "cube"),
        P("cube", "front", None),
        P("cube", "front"),
        P("cube", "front"),
        P("cube", "front", None),
        P("cube", "front"),
        P("cube", "front"),
        P(),
        P("cube", "front"),
    )
    out_specs = (P("cube", "front", None), P(("cube", "front"), None), P("cube", "front"))
    return jax.shard_map(local, mesh=mesh, in_specs=in_specs, out_specs=out_specs, check_vma=False)
```

```python
import functools

import jax
import jax.numpy as jnp
from jax import lax
from jax.experimental import pallas as pl
from jax.experimental.pallas import tpu as pltpu
from jax.sharding import PartitionSpec as P

NU = 2048
PIV = 128
KU = 256
QUARTER = NU // 4
HALF = NU // 2

HIGHEST = lax.Precision.HIGHEST
F32 = jnp.float32
BF16 = jnp.bfloat16
AXES = ("cube", "front")
NN = (((1,), (0,)), ((), ()))
NT = (((1,), (1,)), ((), ()))


def mm(a, b, dims=NN):
    return lax.dot_general(a, b, dims, preferred_element_type=F32)


def exact(a, b, dims=NN):
    return lax.dot_general(a, b, dims, preferred_element_type=F32, precision=HIGHEST)


def split(x):
    high = x.astype(BF16)
    return high, (x - high.astype(F32)).astype(BF16)


def split3(x):
    high = x.astype(BF16)
    rest = x - high.astype(F32)
    mid = rest.astype(BF16)
    return high, mid, (rest - mid.astype(F32)).astype(BF16)


def mm3(a, b, dims=NN):
    ah, al = split(a)
    bh, bl = split(b)
    return mm(ah, bh, dims) + (mm(ah, bl, dims) + mm(al, bh, dims))


def iota(shape, axis):
    return lax.broadcasted_iota(jnp.int32, shape, axis)


def onehot(mask):
    return jnp.where(mask, 1.0, 0.0).astype(BF16)


def newton_inverse(block):
    size = block.shape[0]
    eye = iota((size, size), 0) == iota((size, size), 1)
    diagonal = jnp.where(eye, block, 0.0)
    row = 1.0 / jnp.sum(diagonal, axis=0, keepdims=True)
    col = 1.0 / jnp.sum(diagonal, axis=1, keepdims=True)
    current = jnp.where(eye, 2.0 * row, 0.0) - col * (block * row)
    return 2.0 * current - exact(current, exact(block, current))


def pack_kernel(capacity, slots, cube_count, blocks, owner, target, out):
    count = blocks.shape[0]
    owners = owner[...]
    named = iota((max(cube_count, 16), count), 0) == owners
    earlier = onehot(iota((count, count), 0) < iota((count, count), 1))
    ranks = mm(onehot(named), earlier)
    rank = jnp.sum(jnp.where(named, ranks, 0.0), axis=0, keepdims=True).astype(jnp.int32)
    first = owners * slots
    spots = iota((cube_count * slots, count), 0)
    place = onehot(spots == first + rank)
    high, mid, low = split3(blocks[...])
    values = mm(place, high) + (mm(place, mid) + mm(place, low))
    tags = jnp.where(spots == first + capacity, target[...].astype(F32), 0.0).astype(BF16)
    lanes = onehot(iota((blocks.shape[1], count), 0) == rank)
    out[...] = values + mm(tags, lanes, NT)


def prepare_kernel(
    where,
    leaf_pivot,
    leaf_coupling,
    signs,
    perturb,
    leaf_map,
    level_map,
    inverse,
    links,
    coupling,
    pivots,
    done,
):
    copies = [
        pltpu.make_async_copy(leaf_pivot, pivots, done.at[0]),
        pltpu.make_async_copy(leaf_coupling, coupling, done.at[1]),
    ]
    for copy in copies:
        copy.start()
    leaves, size, _ = pivots.shape
    eye = iota((size, size), 0) == iota((size, size), 1)
    table = level_map[pl.ds(where[4], 1), :]
    rows = iota((16, NU), 0)
    digits = jnp.where(rows == 0, table // 256, jnp.where(rows == 1, table % 256, 0))
    digits = digits.astype(F32).astype(BF16)
    links[...] = jnp.zeros(links.shape, F32)
    for leaf in range(leaves):
        found = mm(digits, onehot(iota((NU, size), 0) == leaf_map[leaf : leaf + 1, :]))
        links[leaf : leaf + 1, :] = found[0:1, :] * 256.0 + found[1:2, :]
    copies[0].wait()
    for leaf in range(leaves):
        shift = signs[leaf : leaf + 1, :].astype(F32) * perturb[leaf : leaf + 1, :]
        inverse[leaf] = newton_inverse(pivots[leaf] + jnp.where(eye, shift, 0.0))
    copies[1].wait()


def places_kernel(where, level_map, out):
    for index, quarter in enumerate((where[3], where[2])):
        start = pl.multiple_of(quarter * QUARTER, QUARTER)
        kept = start + iota((1, QUARTER), 1) >= KU
        for other in range(2):
            group = where[4] + other * (1 - 2 * where[1])
            target = level_map[pl.ds(group, 1), pl.ds(start, QUARTER)] - start
            target = jnp.where(kept, target, -1)
            out[2 * other + index] = onehot(iota((QUARTER, QUARTER), 0) == target)


def leaf_kernel(capacity, slots, cube_count, got, inverse, links, coupling, factor, sent):
    leaves, rows, width = coupling.shape

    def arrivals(cube):
        block = got[cube]
        tags = block[capacity : capacity + 1, :].astype(jnp.int32)
        here = (iota((leaves * rows, width), 0) == tags) & (iota((leaves * rows, width), 1) < capacity)
        values = block
        if slots < width:
            values = jnp.concatenate([block, jnp.zeros((width - slots, width), F32)], axis=0)
        return onehot(here), values

    if cube_count <= 16:
        pairs = [arrivals(cube) for cube in range(cube_count)]
        place = jnp.concatenate([here for here, _ in pairs], axis=1)
        high, mid, low = split3(jnp.concatenate([values for _, values in pairs], axis=0))
        added = mm(place, high) + (mm(place, mid) + mm(place, low))
    else:

        def step(cube, total):
            here, values = arrivals(cube)
            high, mid, low = split3(values)
            return total + (mm(here, high) + (mm(here, mid) + mm(here, low)))

        added = lax.fori_loop(0, cube_count, step, jnp.zeros((leaves * rows, width), F32))
    for leaf in range(leaves):
        rhs = coupling[leaf] + added[leaf * rows : (leaf + 1) * rows, :]
        part = exact(rhs, inverse[leaf])
        factor[leaf] = part
        sent[leaf, 0:rows, :] = -mm3(part, rhs, NT)
        sent[leaf, rows : rows + 8, :] = jnp.where(
            iota((8, width), 0) == 0, links[leaf : leaf + 1, :], 0.0
        )


def panel_parts(pivots):
    upper = newton_inverse(pivots[0:PIV, 0:PIV])
    below = pivots[PIV:KU, 0:PIV]
    lower = newton_inverse(
        pivots[PIV:KU, PIV:KU] - exact(exact(below, upper), below, NT)
    )
    return upper, below, lower


def panel_rows(rows, first, upper, below, lower):
    position = first + iota((rows.shape[0], PIV), 0)
    left = jnp.where(position >= PIV, mm3(rows[:, 0:PIV], upper), 0.0)
    right = rows[:, PIV:KU] - mm3(left, below, NT)
    last = jnp.where(position >= KU, mm3(right, lower), 0.0)
    keep = jnp.concatenate(
        [jnp.where(position >= PIV, rows[:, 0:PIV], 0.0), jnp.where(position >= KU, right, 0.0)], axis=1
    )
    return jnp.concatenate([left, last], axis=1), keep


def mid_kernel(
    where, front, from_x, from_y, from_core, pair, far, factor, left, cols, send, rows
):
    low, high, pos = where[0], where[1], where[2]
    is_low = low == 0

    @pl.when(pos == 0)
    def _():
        rows[...] = front[:, 0:KU].astype(F32)

    @pl.when(pos == 2)
    def _():
        rows[...] = from_x[0:HALF, :]

    @pl.when(pos % 2 == 1)
    def _():
        rows[...] = from_core[0:HALF, :]

    own_cols = pl.multiple_of((pos % 2) * QUARTER, QUARTER)
    held = (pos // 2) == low
    other_cols = jnp.where(
        pos == 0,
        from_y[0:QUARTER, :],
        jnp.where(
            pos == 1, from_core[HALF + QUARTER : NU, :], jnp.where(pos == 2, pair[...], far[...])
        ),
    )
    col_rows = jnp.where(held, rows[pl.ds(own_cols, QUARTER), :], other_cols)
    other_pivots = jnp.where(pos == 1, from_core[NU:, :], other_cols[0:KU, :])
    pivots = jnp.where(is_low, rows[0:KU, :], other_pivots)
    upper, below, lower = panel_parts(pivots)
    row_left, _ = panel_rows(rows[...], low * HALF, upper, below, lower)
    _, col_keep = panel_rows(col_rows, pos * QUARTER, upper, below, lower)
    left[...] = row_left
    cols[...] = col_keep
    slab = HALF // 4
    factor[...] = left[pl.ds(pl.multiple_of(pos * slab, slab), slab), :]
    start = pl.multiple_of((1 - high) * QUARTER, QUARTER)
    send[...] = front[pl.ds(start, QUARTER), :].astype(F32) - mm3(
        left[pl.ds(start, QUARTER), :], col_keep, NT
    )


def spread(values, places, other):
    high, low = split(values)
    row_place, col_place = places[2 * other], places[2 * other + 1]
    high, low = split(mm(row_place, high) + mm(row_place, low))
    return mm(high, col_place, NT) + mm(low, col_place, NT)


def own_kernel(where, front, left, cols, places, out):
    start = pl.multiple_of(where[1] * QUARTER, QUARTER)
    block = front[pl.ds(start, QUARTER), :].astype(F32) - mm3(
        left[pl.ds(start, QUARTER), :], cols[...], NT
    )
    out[...] = spread(block, places, 0)


def other_kernel(block, places, base, out):
    out[...] = base[...] + spread(block[...], places, 1)


def top_kernel(where, front, rows, here, from_y, base, out):
    low, pos, quarter = where[0], where[2], where[3]
    col_rows = jnp.where(low == pos // 2, here[0:QUARTER, :], from_y[0:QUARTER, :])
    pivots = jnp.where(low == 0, here[QUARTER:, :], from_y[QUARTER:, :])
    upper, below, lower = panel_parts(pivots)
    row_left, _ = panel_rows(rows[...], quarter * QUARTER, upper, below, lower)
    _, col_keep = panel_rows(col_rows, pos * QUARTER, upper, below, lower)
    out[...] = base[...] + front[...].astype(F32) - mm3(row_left, col_keep, NT)


def gather_kernel(count, where, *refs):
    sources, base, out = refs[0:count], refs[count], refs[count + 1]
    row_first = where[3] * QUARTER
    col_first = where[2] * QUARTER
    units = [source.at[unit] for source in sources for unit in range(source.shape[0])]
    leaves, _, width = units[0].shape
    total = base[...]
    spots = iota((QUARTER, width), 0)
    for first in range(0, len(units), 2):
        places, highs, lows = [], [], []
        for unit in units[first : first + 2]:
            for leaf in range(leaves):
                link = unit[leaf, width : width + 1, :].astype(jnp.int32)
                places.append(onehot(spots == link - row_first))
                cols = onehot(spots == link - col_first)
                high, low = split(unit[leaf, 0:width, :])
                high, low = split(mm(high, cols, NT) + mm(low, cols, NT))
                highs.append(high)
                lows.append(low)
        place = jnp.concatenate(places, axis=1)
        total = total + (
            mm(place, jnp.concatenate(highs, axis=0)) + mm(place, jnp.concatenate(lows, axis=0))
        )
    out[...] = total


def gather_kernel_of(count):
    return functools.partial(gather_kernel, count)


def stack_kernel(count, *refs):
    first = 0
    for part in refs[0:count]:
        refs[count][first : first + part.shape[0]] = part[...]
        first += part.shape[0]


def stack(parts, after):
    shape = (sum(part.shape[0] for part in parts),) + parts[0].shape[1:]
    return call(functools.partial(stack_kernel, len(parts)), [shape], parts, after, scalars=False)


def cast_kernel(mid_front, top_front, both, mid_cols, mid_part, top_part, done):
    copies = [
        pltpu.make_async_copy(front.at[:, pl.ds(0, KU)], part, done.at[index])
        for index, (front, part) in enumerate(((mid_front, mid_part), (top_front, top_part)))
    ]
    for copy in copies:
        copy.start()
    copies[0].wait()
    values = mid_part[...].astype(F32)
    mid_cols[...] = values
    both[0:HALF, :] = values
    copies[1].wait()
    both[HALF:, :] = top_part[...].astype(F32)


def relay_kernel(where, both, from_x, from_y, core, far, pair):
    core[0 : HALF + QUARTER, :] = jnp.where(where[2] == 0, both[...], from_x[...])
    core[HALF + QUARTER : NU, :] = from_y[QUARTER:HALF, :]
    core[NU:, :] = from_y[0:KU, :]
    far[...] = jnp.where(where[0] == 0, from_y[QUARTER:HALF, :], from_y[0:QUARTER, :])
    pair[...] = from_x[0:QUARTER, :]


def choose_kernel(where, both, from_x, from_core, out):
    pos = where[2]
    held = jnp.where(pos == 0, both[HALF:, :], from_x[HALF:, :])
    out[...] = jnp.where(pos % 2 == 0, held, from_core[HALF : HALF + QUARTER, :])


def pair_kernel(where, top_rows, top_z, out):
    first = where[1] == 0
    even = jnp.where(first, top_rows[...], top_z[...])
    odd = jnp.where(first, top_z[...], top_rows[...])
    out[0:QUARTER, :] = jnp.where(where[2] % 2 == 0, even, odd)
    out[QUARTER:, :] = even[0:KU, :]


def slices_kernel(from_y, from_x, out_x, out_y):
    out_x[...] = from_y[0:1]
    out_y[...] = from_x[1:2]


COST = pl.CostEstimate(flops=10**9, bytes_accessed=1000, transcendentals=0)
FENCE = pl.CostEstimate(flops=10**11, bytes_accessed=1000, transcendentals=0)


def call(body, outs, args, after=(), scalars=True, scratch=(), fence=False, far=(), kind=F32):
    specs = [pl.BlockSpec(memory_space=pltpu.VMEM) for _ in args]
    if scalars:
        specs[0] = pl.BlockSpec(memory_space=pltpu.SMEM)
    for index in far:
        specs[index] = pl.BlockSpec(memory_space=pltpu.HBM)
    given = len(args)
    skipped = len(after)

    def kernel(*refs):
        body(*refs[:given], *refs[given + skipped :])

    shapes = [jax.ShapeDtypeStruct(shape, kind) for shape in outs]
    single = len(shapes) == 1
    return pl.pallas_call(
        kernel,
        out_shape=shapes[0] if single else shapes,
        in_specs=specs + [pl.BlockSpec(memory_space=pl.ANY) for _ in after],
        out_specs=(
            pl.BlockSpec(memory_space=pltpu.VMEM)
            if single
            else [pl.BlockSpec(memory_space=pltpu.VMEM) for _ in shapes]
        ),
        scratch_shapes=list(scratch),
        compiler_params=pltpu.CompilerParams(vmem_limit_bytes=24 * 2**20),
        cost_estimate=FENCE if fence else COST,
    )(*args, *after)


def local(
    kkt_blocks,
    kkt_owner,
    kkt_target,
    leaf_pivot,
    pivot_signs,
    perturb,
    leaf_coupling,
    leaf_map,
    mid_front,
    level_map,
    top_front,
):
    cube_count = lax.axis_size("cube")
    front_count = lax.axis_size("front")
    cube = lax.axis_index("cube")
    front = lax.axis_index("front")
    b0 = cube % 2
    b1 = cube // 2 % 2
    quarter = 2 * b0 + b1
    where = jnp.stack([b0, b1, front, quarter, cube // 2]).astype(jnp.int32)

    def move(array, rule):
        pairs = []
        for source_cube in range(cube_count):
            for source_front in range(front_count):
                target = rule(source_cube % 2, source_cube // 2 % 2, source_front)
                if target is not None:
                    new_cube = source_cube // 4 * 4 + 2 * target[1] + target[0]
                    pairs.append(
                        (source_cube * front_count + source_front, new_cube * front_count + target[2])
                    )
        return lax.ppermute(array, AXES, pairs)

    blocks = kkt_blocks[0]
    block_count, width = blocks.shape
    capacity = max(2, 2 * block_count // cube_count)
    slots = -(-(capacity + 1) // 8) * 8

    both, mid_cols = call(
        cast_kernel,
        [(HALF + QUARTER, KU), (HALF, KU)],
        [mid_front, top_front],
        scalars=False,
        scratch=[
            pltpu.VMEM((HALF, KU), BF16),
            pltpu.VMEM((QUARTER, KU), BF16),
            pltpu.SemaphoreType.DMA((2,)),
        ],
        far=(0, 1),
    )
    both_x = move(both, lambda y, z, f: (y, z, 2) if f == 0 else None)
    mid_y = move(mid_cols, lambda y, z, f: (1 - y, z, 0) if f == 0 else None)

    packed = call(
        functools.partial(pack_kernel, capacity, slots, cube_count),
        [(cube_count * slots, width)],
        [blocks, kkt_owner.reshape(1, block_count), kkt_target.reshape(1, block_count)],
        [both],
        scalars=False,
    )
    got = lax.all_to_all(
        packed.reshape(cube_count, slots, width), "cube", split_axis=0, concat_axis=0, tiled=True
    )

    places = call(
        places_kernel, [(4, QUARTER, QUARTER)], [where, level_map], [packed], kind=BF16
    )
    leaves = leaf_pivot.shape[0]
    size = leaf_pivot.shape[2]
    inverse, links, coupling = call(
        prepare_kernel,
        [(leaves, size, size), (8, size), leaf_coupling.shape],
        [where, leaf_pivot, leaf_coupling, pivot_signs, perturb, leaf_map, level_map],
        [places],
        scratch=[pltpu.VMEM(leaf_pivot.shape, F32), pltpu.SemaphoreType.DMA((2,))],
        far=(1, 2),
    )

    factor, sent = call(
        functools.partial(leaf_kernel, capacity, slots, cube_count),
        [leaf_coupling.shape, (leaves, size + 8, size)],
        [got, inverse, links, coupling],
        scalars=False,
    )
    sent = sent[None]
    k_z = move(sent, lambda y, z, f: (y, 1 - z, f))

    to_core, to_far, to_pair = call(
        relay_kernel,
        [(NU + KU, KU), (QUARTER, KU), (QUARTER, KU)],
        [where, both, both_x, mid_y],
        [sent],
    )
    mid_pair = move(to_pair, lambda y, z, f: (1 - y, z, 2) if f == 2 else None)
    mid_far = move(to_far, lambda y, z, f: (y, z, 3) if f == 0 else None)
    mid_core = move(to_core, lambda y, z, f: (y, z, f + 1) if f % 2 == 0 else None)
    k_own = stack([sent, k_z], [to_core])
    k_x = move(k_own, lambda y, z, f: (y, z, f ^ 2))
    k_y = move(k_own, lambda y, z, f: (1 - y, z, f))
    top_rows = call(choose_kernel, [(QUARTER, KU)], [where, both, both_x, mid_core], [k_own])
    top_z = move(top_rows, lambda y, z, f: (y, 1 - z, f))

    mid_factor, mid_left, mid_keep, mid_send = call(
        mid_kernel,
        [(HALF // front_count, KU), (HALF, KU), (QUARTER, KU), (QUARTER, QUARTER)],
        [where, mid_front, both_x, mid_y, mid_core, mid_pair, mid_far],
        [top_rows],
        scratch=[pltpu.VMEM((HALF, KU), F32)],
    )
    mid_other = move(mid_send, lambda y, z, f: (y, 1 - z, f))

    square = [(QUARTER, QUARTER)]
    to_x, to_y = call(
        slices_kernel, [sent.shape, sent.shape], [k_y, k_x], [mid_send], scalars=False
    )
    k_xy = move(to_x, lambda y, z, f: (y, z, f ^ 2))
    k_yx = move(to_y, lambda y, z, f: (1 - y, z, f))
    here = call(pair_kernel, [(QUARTER + KU, KU)], [where, top_rows, top_z], [to_x])
    top_y = move(here, lambda y, z, f: (1 - y, z, f))
    upper = call(own_kernel, square, [where, mid_front, mid_left, mid_keep, places], [here])
    upper = call(gather_kernel_of(3), square, [where, k_own, k_x, k_y, upper])
    units = stack([k_own, k_x, k_y, k_xy, k_yx], [upper])
    swapped = move(units, lambda y, z, f: (y, z, f ^ 1))
    upper = call(gather_kernel_of(2), square, [where, k_xy, k_yx, upper], [units], fence=True)
    upper = call(gather_kernel_of(1), square, [where, swapped, upper])
    upper = call(top_kernel, square, [where, top_front, top_rows, here, top_y, upper])
    upper = call(other_kernel, square, [mid_other, places, upper], scalars=False)
    return factor, mid_factor, upper


def solution(mesh):
    in_specs = (
        P("front", "cube", None),
        P("front", "cube", None),
        P("front", "cube"),
        P("cube", "front", None),
        P("cube", "front"),
        P("cube", "front"),
        P("cube", "front", None),
        P("cube", "front"),
        P("cube", "front"),
        P(),
        P("cube", "front"),
    )
    out_specs = (P("cube", "front", None), P(("cube", "front"), None), P("cube", "front"))
    return jax.shard_map(local, mesh=mesh, in_specs=in_specs, out_specs=out_specs, check_vma=False)
```

```python
import functools

import jax
import jax.numpy as jnp
from jax import lax
from jax.experimental import pallas as pl
from jax.experimental.pallas import tpu as pltpu
from jax.sharding import PartitionSpec as P

NU = 2048
PIV = 128
KU = 256
QUARTER = NU // 4
HALF = NU // 2

F32 = jnp.float32
BF16 = jnp.bfloat16
AXES = ("cube", "front")
NN = (((1,), (0,)), ((), ()))
NT = (((1,), (1,)), ((), ()))


def mm(a, b, dims=NN):
    return lax.dot_general(a, b, dims, preferred_element_type=F32)


def split(x):
    high = x.astype(BF16)
    return high, (x - high.astype(F32)).astype(BF16)


def split3(x):
    high = x.astype(BF16)
    rest = x - high.astype(F32)
    mid = rest.astype(BF16)
    return high, mid, (rest - mid.astype(F32)).astype(BF16)


def mm3(a, b, dims=NN):
    ah, al = split(a)
    bh, bl = split(b)
    rows = dims[0][1][0]
    return mm(
        jnp.concatenate([ah, ah, al], axis=1), jnp.concatenate([bh, bl, bh], axis=rows), dims
    )


def pick_rows(places, values):
    high, low = split(values)
    return mm(jnp.concatenate([places, places], axis=1), jnp.concatenate([high, low], axis=0))


def pick_cols(values, places):
    high, low = split(values)
    return mm(
        jnp.concatenate([high, low], axis=1), jnp.concatenate([places, places], axis=1), NT
    )


def iota(shape, axis):
    return lax.broadcasted_iota(jnp.int32, shape, axis)


def onehot(mask):
    return jnp.where(mask, 1.0, 0.0).astype(BF16)


def newton_inverse(block):
    size = block.shape[0]
    eye = iota((size, size), 0) == iota((size, size), 1)
    diagonal = jnp.where(eye, block, 0.0)
    row = 1.0 / jnp.sum(diagonal, axis=0, keepdims=True)
    col = 1.0 / jnp.sum(diagonal, axis=1, keepdims=True)
    current = jnp.where(eye, 2.0 * row, 0.0) - col * (block * row)
    return 2.0 * current - mm3(current, mm3(block, current))


def pack_kernel(capacity, slots, cube_count, blocks, owner, target, out):
    count = blocks.shape[0]
    owners = owner[...]
    named = iota((max(cube_count, 16), count), 0) == owners
    earlier = onehot(iota((count, count), 0) < iota((count, count), 1))
    ranks = mm(onehot(named), earlier)
    rank = jnp.sum(jnp.where(named, ranks, 0.0), axis=0, keepdims=True).astype(jnp.int32)
    first = owners * slots
    spots = iota((cube_count * slots, count), 0)
    place = onehot(spots == first + rank)
    high, mid, low = split3(blocks[...])
    values = mm(place, high) + (mm(place, mid) + mm(place, low))
    tags = jnp.where(spots == first + capacity, target[...].astype(F32), 0.0).astype(BF16)
    lanes = onehot(iota((blocks.shape[1], count), 0) == rank)
    out[...] = values + mm(tags, lanes, NT)


def prepare_kernel(
    where,
    leaf_pivot,
    leaf_coupling,
    signs,
    perturb,
    leaf_map,
    level_map,
    inverse,
    links,
    coupling,
    pivots,
    done,
):
    copies = [
        pltpu.make_async_copy(leaf_pivot, pivots, done.at[0]),
        pltpu.make_async_copy(leaf_coupling, coupling, done.at[1]),
    ]
    for copy in copies:
        copy.start()
    leaves, size, _ = pivots.shape
    eye = iota((size, size), 0) == iota((size, size), 1)
    table = level_map[pl.ds(where[4], 1), :]
    rows = iota((16, NU), 0)
    digits = jnp.where(rows == 0, table // 256, jnp.where(rows == 1, table % 256, 0))
    digits = digits.astype(F32).astype(BF16)
    links[...] = jnp.zeros(links.shape, F32)
    for leaf in range(leaves):
        found = mm(digits, onehot(iota((NU, size), 0) == leaf_map[leaf : leaf + 1, :]))
        links[leaf : leaf + 1, :] = found[0:1, :] * 256.0 + found[1:2, :]
    copies[0].wait()
    for leaf in range(leaves):
        shift = signs[leaf : leaf + 1, :].astype(F32) * perturb[leaf : leaf + 1, :]
        inverse[leaf] = newton_inverse(pivots[leaf] + jnp.where(eye, shift, 0.0))
    copies[1].wait()


def places_kernel(where, level_map, out):
    for index, quarter in enumerate((where[3], where[2])):
        start = pl.multiple_of(quarter * QUARTER, QUARTER)
        kept = start + iota((1, QUARTER), 1) >= KU
        for other in range(2):
            group = where[4] + other * (1 - 2 * where[1])
            target = level_map[pl.ds(group, 1), pl.ds(start, QUARTER)] - start
            target = jnp.where(kept, target, -1)
            out[2 * other + index] = onehot(iota((QUARTER, QUARTER), 0) == target)


def leaf_kernel(capacity, slots, cube_count, got, inverse, links, coupling, factor, sent):
    leaves, rows, width = coupling.shape

    def arrivals(cube):
        block = got[cube]
        tags = block[capacity : capacity + 1, :].astype(jnp.int32)
        here = (iota((leaves * rows, width), 0) == tags) & (iota((leaves * rows, width), 1) < capacity)
        values = block
        if slots < width:
            values = jnp.concatenate([block, jnp.zeros((width - slots, width), F32)], axis=0)
        return onehot(here), values

    if cube_count <= 16:
        pairs = [arrivals(cube) for cube in range(cube_count)]
        place = jnp.concatenate([here for here, _ in pairs], axis=1)
        high, mid, low = split3(jnp.concatenate([values for _, values in pairs], axis=0))
        added = mm(place, high) + (mm(place, mid) + mm(place, low))
    else:

        def step(cube, total):
            here, values = arrivals(cube)
            high, mid, low = split3(values)
            return total + (mm(here, high) + (mm(here, mid) + mm(here, low)))

        added = lax.fori_loop(0, cube_count, step, jnp.zeros((leaves * rows, width), F32))
    for leaf in range(leaves):
        rhs = coupling[leaf] + added[leaf * rows : (leaf + 1) * rows, :]
        part = mm3(rhs, inverse[leaf])
        factor[leaf] = part
        sent[leaf, 0:rows, :] = -mm3(part, rhs, NT)
        sent[leaf, rows : rows + 8, :] = jnp.where(
            iota((8, width), 0) == 0, links[leaf : leaf + 1, :], 0.0
        )


def panel_parts(first, below, last):
    upper = newton_inverse(first)
    lower = newton_inverse(last - mm3(mm3(below, upper), below, NT))
    return upper, below, lower


def panel_rows(rows, first, upper, below, lower):
    position = first + iota((rows.shape[0], PIV), 0)
    left = jnp.where(position >= PIV, mm3(rows[:, 0:PIV], upper), 0.0)
    right = rows[:, PIV:KU] - mm3(left, below, NT)
    last = jnp.where(position >= KU, mm3(right, lower), 0.0)
    keep = jnp.concatenate(
        [jnp.where(position >= PIV, rows[:, 0:PIV], 0.0), jnp.where(position >= KU, right, 0.0)], axis=1
    )
    return jnp.concatenate([left, last], axis=1), keep


def mid_kernel(
    where, front, both, from_x, from_y, from_core, cross, left, cols, parts, send, rows
):
    low, high, pos = where[0], where[1], where[2]

    @pl.when(pos == 0)
    def _():
        rows[...] = both[0:HALF, :]

    @pl.when(pos == 2)
    def _():
        rows[...] = from_x[0:HALF, :]

    @pl.when(pos % 2 == 1)
    def _():
        rows[...] = from_core[0:HALF, :]

    own_cols = pl.multiple_of((pos % 2) * QUARTER, QUARTER)
    other_cols = jnp.where(
        pos == 0,
        from_y[0:QUARTER, :],
        jnp.where(pos == 1, from_core[HALF : HALF + QUARTER, :], cross[...]),
    )
    col_rows = jnp.where(pos // 2 == low, rows[pl.ds(own_cols, QUARTER), :], other_cols)
    other_pivots = jnp.where(pos == 1, from_core[HALF + QUARTER :, :], other_cols[0:KU, :])
    pivots = jnp.where(low == 0, rows[0:KU, :], other_pivots)
    upper, below, lower = panel_parts(
        pivots[0:PIV, 0:PIV], pivots[PIV:KU, 0:PIV], pivots[PIV:KU, PIV:KU]
    )
    parts[0], parts[1], parts[2] = upper, below, lower
    _, col_keep = panel_rows(col_rows, pos * QUARTER, upper, below, lower)
    cols[...] = col_keep
    start = pl.multiple_of((1 - high) * QUARTER, QUARTER)
    row_left, _ = panel_rows(
        rows[pl.ds(start, QUARTER), :], low * HALF + start, upper, below, lower
    )
    left[...] = row_left
    send[...] = front[pl.ds(start, QUARTER), :].astype(F32) - mm3(row_left, col_keep, NT)


def spread(values, places, other):
    row_place, col_place = places[2 * other], places[2 * other + 1]
    return pick_cols(pick_rows(row_place, values), col_place)


def own_kernel(
    where, front, both, from_x, from_core, left, cols, parts, places, factor, out, own
):
    low, high, pos = where[0], where[1], where[2]
    start = pl.multiple_of(high * QUARTER, QUARTER)
    here = pl.ds(start, QUARTER)
    rows = jnp.where(
        pos == 0, both[here, :], jnp.where(pos == 2, from_x[here, :], from_core[here, :])
    )
    row_left, _ = panel_rows(rows, low * HALF + start, parts[0], parts[1], parts[2])
    own[...] = row_left
    slab = factor.shape[0]
    first = pos * slab
    inner = pl.ds(pl.multiple_of(first % QUARTER, slab), slab)
    factor[...] = jnp.where(first // QUARTER == high, own[inner, :], left[inner, :])
    block = front[here, :].astype(F32) - mm3(row_left, cols[...], NT)
    out[...] = spread(block, places, 0)


def other_kernel(block, places, base, out):
    out[...] = base[...] + spread(block[...], places, 1)


def top_kernel(where, front, rows, here, from_y, base, out):
    low, pos, quarter = where[0], where[2], where[3]
    col_rows = jnp.where(low == pos // 2, here[0:QUARTER, :], from_y[0:QUARTER, :])
    pivots = jnp.where(low == 0, here[QUARTER:, :], from_y[QUARTER:, :])
    last = jnp.concatenate([pivots[PIV:, 0:PIV], pivots[PIV:, PIV:KU]], axis=0)
    upper, below, lower = panel_parts(pivots[0:PIV, 0:PIV], pivots[0:PIV, PIV:KU], last)
    row_left, _ = panel_rows(rows[...], quarter * QUARTER, upper, below, lower)
    _, col_keep = panel_rows(col_rows, pos * QUARTER, upper, below, lower)
    out[...] = base[...] + front[...].astype(F32) - mm3(row_left, col_keep, NT)


def gather_kernel(count, where, *refs):
    sources, out = refs[0:count], refs[-1]
    row_first = where[3] * QUARTER
    col_first = where[2] * QUARTER
    units = [source.at[unit] for source in sources for unit in range(source.shape[0])]
    leaves, _, width = units[0].shape
    total = refs[count][...] if len(refs) > count + 1 else jnp.zeros(out.shape, F32)
    spots = iota((QUARTER, width), 0)
    for first in range(0, len(units), 2):
        row_places, blocks = [], []
        for unit in units[first : first + 2]:
            for leaf in range(leaves):
                link = unit[leaf, width : width + 1, :].astype(jnp.int32)
                row_places.append(onehot(spots == link - row_first))
                col_places = onehot(spots == link - col_first)
                blocks.append(pick_cols(unit[leaf, 0:width, :], col_places))
        total = total + pick_rows(
            jnp.concatenate(row_places, axis=1), jnp.concatenate(blocks, axis=0)
        )
    out[...] = total


def gather_kernel_of(count):
    return functools.partial(gather_kernel, count)


def stack_kernel(count, *refs):
    first = 0
    for part in refs[0:count]:
        refs[count][first : first + part.shape[0]] = part[...]
        first += part.shape[0]


def stack(parts, after):
    shape = (sum(part.shape[0] for part in parts),) + parts[0].shape[1:]
    return call(functools.partial(stack_kernel, len(parts)), [shape], parts, after, scalars=False)


def cast_kernel(mid_front, top_front, both, mid_cols, mid_part, top_part, done):
    copies = [
        pltpu.make_async_copy(front.at[:, pl.ds(0, KU)], part, done.at[index])
        for index, (front, part) in enumerate(((mid_front, mid_part), (top_front, top_part)))
    ]
    for copy in copies:
        copy.start()
    copies[0].wait()
    values = mid_part[...].astype(F32)
    mid_cols[...] = values
    both[0:HALF, :] = values
    copies[1].wait()
    both[HALF:, :] = top_part[...].astype(F32)


def relay_kernel(where, both, from_x, from_y, core, cross):
    here = where[2] == 0
    core[0:HALF, :] = jnp.where(here, both[0:HALF, :], from_x[0:HALF, :])
    core[HALF : HALF + QUARTER, :] = from_y[QUARTER:HALF, :]
    core[HALF + QUARTER :, :] = from_y[0:KU, :]
    far = jnp.where(where[0] == 0, from_y[QUARTER:HALF, :], from_y[0:QUARTER, :])
    cross[...] = jnp.where(here, far, from_x[0:QUARTER, :])


def choose_kernel(where, both, from_x, out):
    out[...] = jnp.where(where[2] == 0, both[HALF:, :], from_x[HALF:, :])


def pair_kernel(where, top_rows, top_z, pair):
    first = where[1] == 0
    pair[0:QUARTER, :] = jnp.where(first, top_rows[...], top_z[...])
    pair[QUARTER:, :] = jnp.where(first, top_z[...], top_rows[...])


def here_kernel(where, pair, from_core, rows, out):
    even = where[2] % 2 == 0
    own = pl.multiple_of(where[1] * QUARTER, QUARTER)
    rows[...] = jnp.where(even, pair[pl.ds(own, QUARTER), :], from_core[pl.ds(own, QUARTER), :])
    out[0:QUARTER, :] = jnp.where(even, pair[0:QUARTER, :], from_core[QUARTER:, :])
    half = PIV // 2
    first = jnp.where(even, pair[0:KU, :], from_core[0:KU, :])
    out[QUARTER : QUARTER + PIV, 0:PIV] = first[0:PIV, 0:PIV]
    out[QUARTER : QUARTER + PIV, PIV:KU] = first[PIV:KU, 0:PIV]
    out[QUARTER + PIV :, 0:PIV] = first[PIV : PIV + half, PIV:KU]
    out[QUARTER + PIV :, PIV:KU] = first[PIV + half : KU, PIV:KU]


COST = pl.CostEstimate(flops=10**9, bytes_accessed=1000, transcendentals=0)
FENCE = pl.CostEstimate(flops=3 * 10**10, bytes_accessed=1000, transcendentals=0)


def call(body, outs, args, after=(), scalars=True, scratch=(), fence=False, far=(), kind=F32):
    specs = [pl.BlockSpec(memory_space=pltpu.VMEM) for _ in args]
    if scalars:
        specs[0] = pl.BlockSpec(memory_space=pltpu.SMEM)
    for index in far:
        specs[index] = pl.BlockSpec(memory_space=pltpu.HBM)
    given = len(args)
    skipped = len(after)

    def kernel(*refs):
        body(*refs[:given], *refs[given + skipped :])

    shapes = [jax.ShapeDtypeStruct(shape, kind) for shape in outs]
    single = len(shapes) == 1
    return pl.pallas_call(
        kernel,
        out_shape=shapes[0] if single else shapes,
        in_specs=specs + [pl.BlockSpec(memory_space=pl.ANY) for _ in after],
        out_specs=(
            pl.BlockSpec(memory_space=pltpu.VMEM)
            if single
            else [pl.BlockSpec(memory_space=pltpu.VMEM) for _ in shapes]
        ),
        scratch_shapes=list(scratch),
        compiler_params=pltpu.CompilerParams(vmem_limit_bytes=24 * 2**20),
        cost_estimate=FENCE if fence else COST,
    )(*args, *after)


def local(
    kkt_blocks,
    kkt_owner,
    kkt_target,
    leaf_pivot,
    pivot_signs,
    perturb,
    leaf_coupling,
    leaf_map,
    mid_front,
    level_map,
    top_front,
):
    cube_count = lax.axis_size("cube")
    front_count = lax.axis_size("front")
    cube = lax.axis_index("cube")
    front = lax.axis_index("front")
    b0 = cube % 2
    b1 = cube // 2 % 2
    quarter = 2 * b0 + b1
    where = jnp.stack([b0, b1, front, quarter, cube // 2]).astype(jnp.int32)

    def move(array, rule):
        pairs = []
        for source_cube in range(cube_count):
            for source_front in range(front_count):
                target = rule(source_cube % 2, source_cube // 2 % 2, source_front)
                if target is not None:
                    new_cube = source_cube // 4 * 4 + 2 * target[1] + target[0]
                    pairs.append(
                        (source_cube * front_count + source_front, new_cube * front_count + target[2])
                    )
        return lax.ppermute(array, AXES, pairs)

    blocks = kkt_blocks[0]
    block_count, width = blocks.shape
    capacity = max(2, 2 * block_count // cube_count)
    slots = -(-(capacity + 1) // 8) * 8

    both, mid_cols = call(
        cast_kernel,
        [(HALF + QUARTER, KU), (HALF, KU)],
        [mid_front, top_front],
        scalars=False,
        scratch=[
            pltpu.VMEM((HALF, KU), BF16),
            pltpu.VMEM((QUARTER, KU), BF16),
            pltpu.SemaphoreType.DMA((2,)),
        ],
        far=(0, 1),
    )
    both_x = move(both, lambda y, z, f: (y, z, 2) if f == 0 else None)
    mid_y = move(mid_cols, lambda y, z, f: (1 - y, z, 0) if f == 0 else None)

    packed = call(
        functools.partial(pack_kernel, capacity, slots, cube_count),
        [(cube_count * slots, width)],
        [blocks, kkt_owner.reshape(1, block_count), kkt_target.reshape(1, block_count)],
        [both],
        scalars=False,
    )
    got = lax.all_to_all(
        packed.reshape(cube_count, slots, width), "cube", split_axis=0, concat_axis=0, tiled=True
    )

    places = call(
        places_kernel, [(4, QUARTER, QUARTER)], [where, level_map], [packed], kind=BF16
    )
    leaves = leaf_pivot.shape[0]
    size = leaf_pivot.shape[2]
    inverse, links, coupling = call(
        prepare_kernel,
        [(leaves, size, size), (8, size), leaf_coupling.shape],
        [where, leaf_pivot, leaf_coupling, pivot_signs, perturb, leaf_map, level_map],
        [places],
        scratch=[pltpu.VMEM(leaf_pivot.shape, F32), pltpu.SemaphoreType.DMA((2,))],
        far=(1, 2),
    )

    top_rows = call(choose_kernel, [(QUARTER, KU)], [where, both, both_x], [inverse])
    top_z = move(top_rows, lambda y, z, f: (y, 1 - z, f) if f % 2 == 0 else None)

    to_core, to_cross = call(
        relay_kernel,
        [(HALF + QUARTER + KU, KU), (QUARTER, KU)],
        [where, both, both_x, mid_y],
        [top_rows, got],
    )
    mid_cross = move(to_cross, lambda y, z, f: {0: (y, z, 3), 2: (1 - y, z, 2)}.get(f))
    mid_core = move(to_core, lambda y, z, f: (y, z, f + 1) if f % 2 == 0 else None)

    factor, sent = call(
        functools.partial(leaf_kernel, capacity, slots, cube_count),
        [leaf_coupling.shape, (leaves, size + 8, size)],
        [got, inverse, links, coupling],
        [to_core],
        scalars=False,
    )
    sent = sent[None]
    k_z = move(sent, lambda y, z, f: (y, 1 - z, f))
    mid_left, mid_keep, mid_parts, mid_send = call(
        mid_kernel,
        [(QUARTER, KU), (QUARTER, KU), (3, PIV, PIV), (QUARTER, QUARTER)],
        [where, mid_front, both, both_x, mid_y, mid_core, mid_cross],
        [sent],
        scratch=[pltpu.VMEM((HALF, KU), F32)],
        fence=True,
    )
    mid_other = move(mid_send, lambda y, z, f: (y, 1 - z, f))

    square = [(QUARTER, QUARTER)]
    k_own = stack([sent, k_z], [mid_send])
    k_x = move(k_own, lambda y, z, f: (y, z, f ^ 2))
    k_y = move(k_own, lambda y, z, f: (1 - y, z, f))
    pair = call(pair_kernel, [(HALF, KU)], [where, top_rows, top_z], [k_own])
    pair_core = move(pair, lambda y, z, f: (y, z, f ^ 1))
    top_own, here = call(
        here_kernel,
        [(QUARTER, KU), (QUARTER + PIV + PIV // 2, KU)],
        [where, pair, pair_core],
    )
    top_y = move(here, lambda y, z, f: (1 - y, z, f))
    mid_factor, upper = call(
        own_kernel,
        [(HALF // front_count, KU), (QUARTER, QUARTER)],
        [where, mid_front, both, both_x, mid_core, mid_left, mid_keep, mid_parts, places],
        [here],
        scratch=[pltpu.VMEM((QUARTER, KU), F32)],
    )
    to_x = stack([k_y], [upper])
    k_xy = move(to_x, lambda y, z, f: (y, z, f ^ 2))
    units = stack([k_own, k_x, k_y], [to_x])
    swapped = move(units, lambda y, z, f: (y, z, f ^ 1))
    upper = call(gather_kernel_of(3), square, [where, k_own, k_x, k_y, upper], [units], fence=True)
    upper = call(gather_kernel_of(1), square, [where, swapped, upper])
    units = stack([k_xy], [upper])
    swapped = move(units, lambda y, z, f: (y, z, f ^ 1))
    upper = call(gather_kernel_of(1), square, [where, k_xy, upper], [units], fence=True)
    upper = call(gather_kernel_of(1), square, [where, swapped, upper])
    upper = call(top_kernel, square, [where, top_front, top_own, here, top_y, upper])
    upper = call(other_kernel, square, [mid_other, places, upper], scalars=False)
    return factor, mid_factor, upper


def solution(mesh):
    in_specs = (
        P("front", "cube", None),
        P("front", "cube", None),
        P("front", "cube"),
        P("cube", "front", None),
        P("cube", "front"),
        P("cube", "front"),
        P("cube", "front", None),
        P("cube", "front"),
        P("cube", "front"),
        P(),
        P("cube", "front"),
    )
    out_specs = (P("cube", "front", None), P(("cube", "front"), None), P("cube", "front"))
    return jax.shard_map(local, mesh=mesh, in_specs=in_specs, out_specs=out_specs, check_vma=False)
```

```python
import functools

import jax
import jax.numpy as jnp
from jax import lax
from jax.experimental import pallas as pl
from jax.experimental.pallas import tpu as pltpu
from jax.sharding import PartitionSpec as P

NU = 2048
PIV = 128
KU = 256
QUARTER = NU // 4
HALF = NU // 2

F32 = jnp.float32
BF16 = jnp.bfloat16
AXES = ("cube", "front")
NN = (((1,), (0,)), ((), ()))
NT = (((1,), (1,)), ((), ()))


def mm(a, b, dims=NN):
    return lax.dot_general(a, b, dims, preferred_element_type=F32)


def split(x):
    high = x.astype(BF16)
    return high, (x - high.astype(F32)).astype(BF16)


def split3(x):
    high = x.astype(BF16)
    rest = x - high.astype(F32)
    mid = rest.astype(BF16)
    return high, mid, (rest - mid.astype(F32)).astype(BF16)


def mm3(a, b, dims=NN):
    ah, al = split(a)
    bh, bl = split(b)
    rows = dims[0][1][0]
    return mm(
        jnp.concatenate([ah, ah, al], axis=1), jnp.concatenate([bh, bl, bh], axis=rows), dims
    )


def pick_rows(places, values):
    high, low = split(values)
    return mm(jnp.concatenate([places, places], axis=1), jnp.concatenate([high, low], axis=0))


def pick_cols(values, places):
    high, low = split(values)
    return mm(
        jnp.concatenate([high, low], axis=1), jnp.concatenate([places, places], axis=1), NT
    )


def iota(shape, axis):
    return lax.broadcasted_iota(jnp.int32, shape, axis)


def onehot(mask):
    return jnp.where(mask, 1.0, 0.0).astype(BF16)


def newton_inverse(block):
    size = block.shape[0]
    eye = iota((size, size), 0) == iota((size, size), 1)
    diagonal = jnp.where(eye, block, 0.0)
    row = 1.0 / jnp.sum(diagonal, axis=0, keepdims=True)
    col = 1.0 / jnp.sum(diagonal, axis=1, keepdims=True)
    current = jnp.where(eye, 2.0 * row, 0.0) - col * (block * row)
    return 2.0 * current - mm3(current, mm3(block, current))


def pack_kernel(capacity, slots, cube_count, blocks, owner, target, out):
    count = blocks.shape[0]
    owners = owner[...]
    named = iota((max(cube_count, 16), count), 0) == owners
    earlier = onehot(iota((count, count), 0) < iota((count, count), 1))
    ranks = mm(onehot(named), earlier)
    rank = jnp.sum(jnp.where(named, ranks, 0.0), axis=0, keepdims=True).astype(jnp.int32)
    first = owners * slots
    spots = iota((cube_count * slots, count), 0)
    place = onehot(spots == first + rank)
    high, mid, low = split3(blocks[...])
    values = mm(place, high) + (mm(place, mid) + mm(place, low))
    tags = jnp.where(spots == first + capacity, target[...].astype(F32), 0.0).astype(BF16)
    lanes = onehot(iota((blocks.shape[1], count), 0) == rank)
    out[...] = values + mm(tags, lanes, NT)


def prepare_kernel(
    where,
    leaf_pivot,
    leaf_coupling,
    signs,
    perturb,
    leaf_map,
    level_map,
    inverse,
    links,
    coupling,
    pivots,
    done,
):
    copies = [
        pltpu.make_async_copy(leaf_pivot, pivots, done.at[0]),
        pltpu.make_async_copy(leaf_coupling, coupling, done.at[1]),
    ]
    for copy in copies:
        copy.start()
    leaves, size, _ = pivots.shape
    eye = iota((size, size), 0) == iota((size, size), 1)
    table = level_map[pl.ds(where[4], 1), :]
    rows = iota((16, NU), 0)
    digits = jnp.where(rows == 0, table // 256, jnp.where(rows == 1, table % 256, 0))
    digits = digits.astype(F32).astype(BF16)
    links[...] = jnp.zeros(links.shape, F32)
    for leaf in range(leaves):
        found = mm(digits, onehot(iota((NU, size), 0) == leaf_map[leaf : leaf + 1, :]))
        links[leaf : leaf + 1, :] = found[0:1, :] * 256.0 + found[1:2, :]
    copies[0].wait()
    for leaf in range(leaves):
        shift = signs[leaf : leaf + 1, :].astype(F32) * perturb[leaf : leaf + 1, :]
        inverse[leaf] = newton_inverse(pivots[leaf] + jnp.where(eye, shift, 0.0))
    copies[1].wait()


def places_kernel(where, level_map, out):
    for index, quarter in enumerate((where[3], where[2])):
        start = pl.multiple_of(quarter * QUARTER, QUARTER)
        kept = start + iota((1, QUARTER), 1) >= KU
        for other in range(2):
            group = where[4] + other * (1 - 2 * where[1])
            target = level_map[pl.ds(group, 1), pl.ds(start, QUARTER)] - start
            target = jnp.where(kept, target, -1)
            out[2 * other + index] = onehot(iota((QUARTER, QUARTER), 0) == target)


def leaf_kernel(capacity, slots, cube_count, got, inverse, links, coupling, factor, sent):
    leaves, rows, width = coupling.shape

    def arrivals(cube):
        block = got[cube]
        tags = block[capacity : capacity + 1, :].astype(jnp.int32)
        here = (iota((leaves * rows, width), 0) == tags) & (iota((leaves * rows, width), 1) < capacity)
        values = block
        if slots < width:
            values = jnp.concatenate([block, jnp.zeros((width - slots, width), F32)], axis=0)
        return onehot(here), values

    if cube_count <= 16:
        pairs = [arrivals(cube) for cube in range(cube_count)]
        place = jnp.concatenate([here for here, _ in pairs], axis=1)
        high, mid, low = split3(jnp.concatenate([values for _, values in pairs], axis=0))
        added = mm(place, high) + (mm(place, mid) + mm(place, low))
    else:

        def step(cube, total):
            here, values = arrivals(cube)
            high, mid, low = split3(values)
            return total + (mm(here, high) + (mm(here, mid) + mm(here, low)))

        added = lax.fori_loop(0, cube_count, step, jnp.zeros((leaves * rows, width), F32))
    for leaf in range(leaves):
        rhs = coupling[leaf] + added[leaf * rows : (leaf + 1) * rows, :]
        part = mm3(rhs, inverse[leaf])
        factor[leaf] = part
        sent[leaf, 0:rows, :] = -mm3(part, rhs, NT)
        sent[leaf, rows : rows + 8, :] = jnp.where(
            iota((8, width), 0) == 0, links[leaf : leaf + 1, :], 0.0
        )


def panel_parts(first, below, last):
    upper = newton_inverse(first)
    lower = newton_inverse(last - mm3(mm3(below, upper), below, NT))
    return upper, below, lower


def panel_rows(rows, first, upper, below, lower):
    position = first + iota((rows.shape[0], PIV), 0)
    left = jnp.where(position >= PIV, mm3(rows[:, 0:PIV], upper), 0.0)
    right = rows[:, PIV:KU] - mm3(left, below, NT)
    last = jnp.where(position >= KU, mm3(right, lower), 0.0)
    keep = jnp.concatenate(
        [jnp.where(position >= PIV, rows[:, 0:PIV], 0.0), jnp.where(position >= KU, right, 0.0)], axis=1
    )
    return jnp.concatenate([left, last], axis=1), keep


def mid_kernel(
    where, front, both, from_x, from_y, from_core, cross, left, cols, parts, send, rows
):
    low, high, pos = where[0], where[1], where[2]

    @pl.when(pos == 0)
    def _():
        rows[...] = both[0:HALF, :]

    @pl.when(pos == 2)
    def _():
        rows[...] = from_x[0:HALF, :]

    @pl.when(pos % 2 == 1)
    def _():
        rows[...] = from_core[0:HALF, :]

    own_cols = pl.multiple_of((pos % 2) * QUARTER, QUARTER)
    other_cols = jnp.where(
        pos == 0,
        from_y[0:QUARTER, :],
        jnp.where(pos == 1, from_core[HALF : HALF + QUARTER, :], cross[...]),
    )
    col_rows = jnp.where(pos // 2 == low, rows[pl.ds(own_cols, QUARTER), :], other_cols)
    other_pivots = jnp.where(pos == 1, from_core[HALF + QUARTER :, :], other_cols[0:KU, :])
    pivots = jnp.where(low == 0, rows[0:KU, :], other_pivots)
    upper, below, lower = panel_parts(
        pivots[0:PIV, 0:PIV], pivots[PIV:KU, 0:PIV], pivots[PIV:KU, PIV:KU]
    )
    parts[0], parts[1], parts[2] = upper, below, lower
    _, col_keep = panel_rows(col_rows, pos * QUARTER, upper, below, lower)
    cols[...] = col_keep
    start = pl.multiple_of((1 - high) * QUARTER, QUARTER)
    row_left, _ = panel_rows(
        rows[pl.ds(start, QUARTER), :], low * HALF + start, upper, below, lower
    )
    left[...] = row_left
    send[...] = front[pl.ds(start, QUARTER), :].astype(F32) - mm3(row_left, col_keep, NT)


def spread(values, places, other):
    row_place, col_place = places[2 * other], places[2 * other + 1]
    return pick_cols(pick_rows(row_place, values), col_place)


def own_kernel(
    where, front, both, from_x, from_core, left, cols, parts, places, factor, out, own
):
    low, high, pos = where[0], where[1], where[2]
    start = pl.multiple_of(high * QUARTER, QUARTER)
    here = pl.ds(start, QUARTER)
    rows = jnp.where(
        pos == 0, both[here, :], jnp.where(pos == 2, from_x[here, :], from_core[here, :])
    )
    row_left, _ = panel_rows(rows, low * HALF + start, parts[0], parts[1], parts[2])
    own[...] = row_left
    slab = factor.shape[0]
    first = pos * slab
    inner = pl.ds(pl.multiple_of(first % QUARTER, slab), slab)
    factor[...] = jnp.where(first // QUARTER == high, own[inner, :], left[inner, :])
    block = front[here, :].astype(F32) - mm3(row_left, cols[...], NT)
    out[...] = spread(block, places, 0)


def other_kernel(block, places, base, out):
    out[...] = base[...] + spread(block[...], places, 1)


def top_kernel(where, front, rows, here, first, from_y, from_core, base, out):
    low, pos, quarter = where[0], where[2], where[3]
    col_rows = jnp.where(low == pos // 2, here[...], from_y[...])
    pivots = jnp.where(
        low == 0, first[...], jnp.where(pos == 1, from_core[...], from_y[0:KU, :])
    )
    upper, below, lower = panel_parts(
        pivots[0:PIV, 0:PIV], pivots[PIV:KU, 0:PIV], pivots[PIV:KU, PIV:KU]
    )
    row_left, _ = panel_rows(rows[...], quarter * QUARTER, upper, below, lower)
    _, col_keep = panel_rows(col_rows, pos * QUARTER, upper, below, lower)
    out[...] = base[...] + front[...].astype(F32) - mm3(row_left, col_keep, NT)


def gather_kernel(count, where, *refs):
    sources, out = refs[0:count], refs[-1]
    row_first = where[3] * QUARTER
    col_first = where[2] * QUARTER
    units = [source.at[unit] for source in sources for unit in range(source.shape[0])]
    leaves, _, width = units[0].shape
    total = refs[count][...] if len(refs) > count + 1 else jnp.zeros(out.shape, F32)
    spots = iota((QUARTER, width), 0)
    for first in range(0, len(units), 2):
        row_places, blocks = [], []
        for unit in units[first : first + 2]:
            for leaf in range(leaves):
                link = unit[leaf, width : width + 1, :].astype(jnp.int32)
                row_places.append(onehot(spots == link - row_first))
                col_places = onehot(spots == link - col_first)
                blocks.append(pick_cols(unit[leaf, 0:width, :], col_places))
        total = total + pick_rows(
            jnp.concatenate(row_places, axis=1), jnp.concatenate(blocks, axis=0)
        )
    out[...] = total


def gather_kernel_of(count):
    return functools.partial(gather_kernel, count)


def stack_kernel(count, *refs):
    first = 0
    for part in refs[0:count]:
        refs[count][first : first + part.shape[0]] = part[...]
        first += part.shape[0]


def stack(parts, after):
    shape = (sum(part.shape[0] for part in parts),) + parts[0].shape[1:]
    return call(functools.partial(stack_kernel, len(parts)), [shape], parts, after, scalars=False)


def cast_kernel(mid_front, top_front, both, mid_cols, mid_part, top_part, done):
    copies = [
        pltpu.make_async_copy(front.at[:, pl.ds(0, KU)], part, done.at[index])
        for index, (front, part) in enumerate(((mid_front, mid_part), (top_front, top_part)))
    ]
    for copy in copies:
        copy.start()
    copies[0].wait()
    values = mid_part[...].astype(F32)
    mid_cols[...] = values
    both[0:HALF, :] = values
    copies[1].wait()
    both[HALF:, :] = top_part[...].astype(F32)


def relay_kernel(where, both, from_x, from_y, core, cross):
    here = where[2] == 0
    core[0:HALF, :] = jnp.where(here, both[0:HALF, :], from_x[0:HALF, :])
    core[HALF : HALF + QUARTER, :] = from_y[QUARTER:HALF, :]
    core[HALF + QUARTER :, :] = from_y[0:KU, :]
    far = jnp.where(where[0] == 0, from_y[QUARTER:HALF, :], from_y[0:QUARTER, :])
    cross[...] = jnp.where(here, far, from_x[0:QUARTER, :])


def choose_kernel(where, both, from_x, out):
    out[...] = jnp.where(where[2] == 0, both[HALF:, :], from_x[HALF:, :])


def pair_kernel(where, top_rows, top_z, pair):
    first = where[1] == 0
    pair[0:QUARTER, :] = jnp.where(first, top_rows[...], top_z[...])
    pair[QUARTER:, :] = jnp.where(first, top_z[...], top_rows[...])


def here_kernel(where, pair, from_core, rows, out, first):
    even = where[2] % 2 == 0
    own = pl.ds(pl.multiple_of(where[1] * QUARTER, QUARTER), QUARTER)
    rows[...] = jnp.where(even, pair[own, :], from_core[own, :])
    low_half = jnp.where(even, pair[0:QUARTER, :], from_core[0:QUARTER, :])
    first[...] = low_half[0:KU, :]
    second = jnp.logical_and(jnp.logical_not(even), where[2] // 2 == where[0])
    out[...] = jnp.where(second, from_core[QUARTER:, :], low_half)


def first_kernel(from_y, out):
    out[...] = from_y[0:KU, :]


COST = pl.CostEstimate(flops=10**9, bytes_accessed=1000, transcendentals=0)
FENCE = pl.CostEstimate(flops=3 * 10**10, bytes_accessed=1000, transcendentals=0)


def call(body, outs, args, after=(), scalars=True, scratch=(), fence=False, far=(), kind=F32):
    specs = [pl.BlockSpec(memory_space=pltpu.VMEM) for _ in args]
    if scalars:
        specs[0] = pl.BlockSpec(memory_space=pltpu.SMEM)
    for index in far:
        specs[index] = pl.BlockSpec(memory_space=pltpu.HBM)
    given = len(args)
    skipped = len(after)

    def kernel(*refs):
        body(*refs[:given], *refs[given + skipped :])

    shapes = [jax.ShapeDtypeStruct(shape, kind) for shape in outs]
    single = len(shapes) == 1
    return pl.pallas_call(
        kernel,
        out_shape=shapes[0] if single else shapes,
        in_specs=specs + [pl.BlockSpec(memory_space=pl.ANY) for _ in after],
        out_specs=(
            pl.BlockSpec(memory_space=pltpu.VMEM)
            if single
            else [pl.BlockSpec(memory_space=pltpu.VMEM) for _ in shapes]
        ),
        scratch_shapes=list(scratch),
        compiler_params=pltpu.CompilerParams(vmem_limit_bytes=24 * 2**20),
        cost_estimate=FENCE if fence else COST,
    )(*args, *after)


def local(
    kkt_blocks,
    kkt_owner,
    kkt_target,
    leaf_pivot,
    pivot_signs,
    perturb,
    leaf_coupling,
    leaf_map,
    mid_front,
    level_map,
    top_front,
):
    cube_count = lax.axis_size("cube")
    front_count = lax.axis_size("front")
    cube = lax.axis_index("cube")
    front = lax.axis_index("front")
    b0 = cube % 2
    b1 = cube // 2 % 2
    quarter = 2 * b0 + b1
    where = jnp.stack([b0, b1, front, quarter, cube // 2]).astype(jnp.int32)

    def move(array, rule):
        pairs = []
        for source_cube in range(cube_count):
            for source_front in range(front_count):
                target = rule(source_cube % 2, source_cube // 2 % 2, source_front)
                if target is not None:
                    new_cube = source_cube // 4 * 4 + 2 * target[1] + target[0]
                    pairs.append(
                        (source_cube * front_count + source_front, new_cube * front_count + target[2])
                    )
        return lax.ppermute(array, AXES, pairs)

    blocks = kkt_blocks[0]
    block_count, width = blocks.shape
    capacity = max(2, 2 * block_count // cube_count)
    slots = -(-(capacity + 1) // 8) * 8

    both, mid_cols = call(
        cast_kernel,
        [(HALF + QUARTER, KU), (HALF, KU)],
        [mid_front, top_front],
        scalars=False,
        scratch=[
            pltpu.VMEM((HALF, KU), BF16),
            pltpu.VMEM((QUARTER, KU), BF16),
            pltpu.SemaphoreType.DMA((2,)),
        ],
        far=(0, 1),
    )
    both_x = move(both, lambda y, z, f: (y, z, 2) if f == 0 else None)
    mid_y = move(mid_cols, lambda y, z, f: (1 - y, z, 0) if f == 0 else None)

    packed = call(
        functools.partial(pack_kernel, capacity, slots, cube_count),
        [(cube_count * slots, width)],
        [blocks, kkt_owner.reshape(1, block_count), kkt_target.reshape(1, block_count)],
        [both],
        scalars=False,
    )
    got = lax.all_to_all(
        packed.reshape(cube_count, slots, width), "cube", split_axis=0, concat_axis=0, tiled=True
    )

    places = call(
        places_kernel, [(4, QUARTER, QUARTER)], [where, level_map], [packed], kind=BF16
    )
    leaves = leaf_pivot.shape[0]
    size = leaf_pivot.shape[2]
    inverse, links, coupling = call(
        prepare_kernel,
        [(leaves, size, size), (8, size), leaf_coupling.shape],
        [where, leaf_pivot, leaf_coupling, pivot_signs, perturb, leaf_map, level_map],
        [places],
        scratch=[pltpu.VMEM(leaf_pivot.shape, F32), pltpu.SemaphoreType.DMA((2,))],
        far=(1, 2),
    )

    to_core, to_cross = call(
        relay_kernel,
        [(HALF + QUARTER + KU, KU), (QUARTER, KU)],
        [where, both, both_x, mid_y],
        [inverse, got],
    )
    mid_cross = move(to_cross, lambda y, z, f: {0: (y, z, 3), 2: (1 - y, z, 2)}.get(f))
    mid_core = move(to_core, lambda y, z, f: (y, z, f + 1) if f % 2 == 0 else None)

    top_rows = call(choose_kernel, [(QUARTER, KU)], [where, both, both_x], [to_core])
    top_z = move(top_rows, lambda y, z, f: (y, 1 - z, f))

    factor, sent = call(
        functools.partial(leaf_kernel, capacity, slots, cube_count),
        [leaf_coupling.shape, (leaves, size + 8, size)],
        [got, inverse, links, coupling],
        [to_core],
        scalars=False,
    )
    sent = sent[None]
    k_z = move(sent, lambda y, z, f: (y, 1 - z, f))
    mid_left, mid_keep, mid_parts, mid_send = call(
        mid_kernel,
        [(QUARTER, KU), (QUARTER, KU), (3, PIV, PIV), (QUARTER, QUARTER)],
        [where, mid_front, both, both_x, mid_y, mid_core, mid_cross],
        [sent],
        scratch=[pltpu.VMEM((HALF, KU), F32)],
        fence=True,
    )
    mid_other = move(mid_send, lambda y, z, f: (y, 1 - z, f))

    square = [(QUARTER, QUARTER)]
    k_own = stack([sent, k_z], [mid_send])
    k_x = move(k_own, lambda y, z, f: (y, z, f ^ 2))
    k_y = move(k_own, lambda y, z, f: (1 - y, z, f))
    pair = call(pair_kernel, [(HALF, KU)], [where, top_rows, top_z], [k_own])
    pair_core = move(pair, lambda y, z, f: (y, z, f ^ 1))
    top_own, here, top_first = call(
        here_kernel,
        [(QUARTER, KU), (QUARTER, KU), (KU, KU)],
        [where, pair, pair_core],
    )
    top_y = move(here, lambda y, z, f: (1 - y, z, f))
    mid_factor, upper = call(
        own_kernel,
        [(HALF // front_count, KU), (QUARTER, QUARTER)],
        [where, mid_front, both, both_x, mid_core, mid_left, mid_keep, mid_parts, places],
        [here],
        scratch=[pltpu.VMEM((QUARTER, KU), F32)],
    )
    to_x = stack([k_y], [upper])
    k_xy = move(to_x, lambda y, z, f: (y, z, f ^ 2))
    units = stack([k_own, k_x, k_y], [to_x])
    swapped = move(units, lambda y, z, f: (y, z, f ^ 1))
    upper = call(gather_kernel_of(3), square, [where, k_own, k_x, k_y, upper], [units], fence=True)
    upper = call(gather_kernel_of(1), square, [where, swapped, upper])
    units = stack([k_xy], [upper])
    swapped = move(units, lambda y, z, f: (y, z, f ^ 1))
    upper = call(gather_kernel_of(1), square, [where, k_xy, upper], [units], fence=True)
    from_y = call(first_kernel, [(KU, KU)], [top_y], [upper], scalars=False)
    top_core = move(from_y, lambda y, z, f: (y, z, f ^ 1))
    upper = call(gather_kernel_of(1), square, [where, swapped, upper], [from_y])
    upper = call(
        top_kernel,
        square,
        [where, top_front, top_own, here, top_first, top_y, top_core, upper],
    )
    upper = call(other_kernel, square, [mid_other, places, upper], scalars=False)
    return factor, mid_factor, upper


def solution(mesh):
    in_specs = (
        P("front", "cube", None),
        P("front", "cube", None),
        P("front", "cube"),
        P("cube", "front", None),
        P("cube", "front"),
        P("cube", "front"),
        P("cube", "front", None),
        P("cube", "front"),
        P("cube", "front"),
        P(),
        P("cube", "front"),
    )
    out_specs = (P("cube", "front", None), P(("cube", "front"), None), P("cube", "front"))
    return jax.shard_map(local, mesh=mesh, in_specs=in_specs, out_specs=out_specs, check_vma=False)
```

```python
import functools

import jax
import jax.numpy as jnp
from jax import lax
from jax.experimental import pallas as pl
from jax.experimental.pallas import tpu as pltpu
from jax.sharding import PartitionSpec as P

NU = 2048
PIV = 128
KU = 256
QUARTER = NU // 4
HALF = NU // 2

F32 = jnp.float32
BF16 = jnp.bfloat16
AXES = ("cube", "front")
NN = (((1,), (0,)), ((), ()))
NT = (((1,), (1,)), ((), ()))


def mm(a, b, dims=NN):
    return lax.dot_general(a, b, dims, preferred_element_type=F32)


def split(x):
    high = x.astype(BF16)
    return high, (x - high.astype(F32)).astype(BF16)


def split3(x):
    high = x.astype(BF16)
    rest = x - high.astype(F32)
    mid = rest.astype(BF16)
    return high, mid, (rest - mid.astype(F32)).astype(BF16)


def mm3(a, b, dims=NN):
    ah, al = split(a)
    bh, bl = split(b)
    rows = dims[0][1][0]
    return mm(
        jnp.concatenate([ah, ah, al], axis=1), jnp.concatenate([bh, bl, bh], axis=rows), dims
    )


def pick_rows(places, values):
    high, low = split(values)
    return mm(jnp.concatenate([places, places], axis=1), jnp.concatenate([high, low], axis=0))


def pick_cols(values, places):
    high, low = split(values)
    return mm(
        jnp.concatenate([high, low], axis=1), jnp.concatenate([places, places], axis=1), NT
    )


def iota(shape, axis):
    return lax.broadcasted_iota(jnp.int32, shape, axis)


def onehot(mask):
    return jnp.where(mask, 1.0, 0.0).astype(BF16)


def newton_inverse(block):
    size = block.shape[0]
    eye = iota((size, size), 0) == iota((size, size), 1)
    diagonal = jnp.where(eye, block, 0.0)
    row = 1.0 / jnp.sum(diagonal, axis=0, keepdims=True)
    col = 1.0 / jnp.sum(diagonal, axis=1, keepdims=True)
    current = jnp.where(eye, 2.0 * row, 0.0) - col * (block * row)
    return 2.0 * current - mm3(current, mm3(block, current))


def pack_kernel(capacity, slots, cube_count, blocks, owner, target, out, token):
    count = blocks.shape[0]
    owners = owner[...]
    named = iota((max(cube_count, 16), count), 0) == owners
    earlier = onehot(iota((count, count), 0) < iota((count, count), 1))
    ranks = mm(onehot(named), earlier)
    rank = jnp.sum(jnp.where(named, ranks, 0.0), axis=0, keepdims=True).astype(jnp.int32)
    first = owners * slots
    spots = iota((cube_count * slots, count), 0)
    place = onehot(spots == first + rank)
    high, mid, low = split3(blocks[...])
    values = mm(place, high) + (mm(place, mid) + mm(place, low))
    tags = jnp.where(spots == first + capacity, target[...].astype(F32), 0.0).astype(BF16)
    lanes = onehot(iota((blocks.shape[1], count), 0) == rank)
    out[...] = values + mm(tags, lanes, NT)
    token[...] = jnp.zeros(token.shape, F32)


def prepare_kernel(
    where,
    leaf_pivot,
    leaf_coupling,
    signs,
    perturb,
    leaf_map,
    level_map,
    inverse,
    links,
    coupling,
    pivots,
    done,
):
    copies = [
        pltpu.make_async_copy(leaf_pivot, pivots, done.at[0]),
        pltpu.make_async_copy(leaf_coupling, coupling, done.at[1]),
    ]
    for copy in copies:
        copy.start()
    leaves, size, _ = pivots.shape
    eye = iota((size, size), 0) == iota((size, size), 1)
    table = level_map[pl.ds(where[4], 1), :]
    rows = iota((16, NU), 0)
    digits = jnp.where(rows == 0, table // 256, jnp.where(rows == 1, table % 256, 0))
    digits = digits.astype(F32).astype(BF16)
    links[...] = jnp.zeros(links.shape, F32)
    for leaf in range(leaves):
        found = mm(digits, onehot(iota((NU, size), 0) == leaf_map[leaf : leaf + 1, :]))
        links[leaf : leaf + 1, :] = found[0:1, :] * 256.0 + found[1:2, :]
    copies[0].wait()
    for leaf in range(leaves):
        shift = signs[leaf : leaf + 1, :].astype(F32) * perturb[leaf : leaf + 1, :]
        inverse[leaf] = newton_inverse(pivots[leaf] + jnp.where(eye, shift, 0.0))
    copies[1].wait()


def places_kernel(where, level_map, out, token):
    for index, quarter in enumerate((where[3], where[2])):
        start = pl.multiple_of(quarter * QUARTER, QUARTER)
        kept = start + iota((1, QUARTER), 1) >= KU
        for other in range(2):
            group = where[4] + other * (1 - 2 * where[1])
            target = level_map[pl.ds(group, 1), pl.ds(start, QUARTER)] - start
            target = jnp.where(kept, target, -1)
            out[2 * other + index] = onehot(iota((QUARTER, QUARTER), 0) == target)
    token[...] = jnp.zeros(token.shape, BF16)


def leaf_kernel(capacity, slots, cube_count, got, inverse, links, coupling, factor, sent):
    leaves, rows, width = coupling.shape

    def arrivals(cube):
        block = got[cube]
        tags = block[capacity : capacity + 1, :].astype(jnp.int32)
        here = (iota((leaves * rows, width), 0) == tags) & (iota((leaves * rows, width), 1) < capacity)
        values = block
        if slots < width:
            values = jnp.concatenate([block, jnp.zeros((width - slots, width), F32)], axis=0)
        return onehot(here), values

    if cube_count <= 16:
        pairs = [arrivals(cube) for cube in range(cube_count)]
        place = jnp.concatenate([here for here, _ in pairs], axis=1)
        high, mid, low = split3(jnp.concatenate([values for _, values in pairs], axis=0))
        added = mm(place, high) + (mm(place, mid) + mm(place, low))
    else:

        def step(cube, total):
            here, values = arrivals(cube)
            high, mid, low = split3(values)
            return total + (mm(here, high) + (mm(here, mid) + mm(here, low)))

        added = lax.fori_loop(0, cube_count, step, jnp.zeros((leaves * rows, width), F32))
    for leaf in range(leaves):
        rhs = coupling[leaf] + added[leaf * rows : (leaf + 1) * rows, :]
        part = mm3(rhs, inverse[leaf])
        factor[leaf] = part
        sent[leaf, 0:rows, :] = -mm3(part, rhs, NT)
        sent[leaf, rows : rows + 8, :] = jnp.where(
            iota((8, width), 0) == 0, links[leaf : leaf + 1, :], 0.0
        )


def panel_parts(first, below, last):
    upper = newton_inverse(first)
    lower = newton_inverse(last - mm3(mm3(below, upper), below, NT))
    return upper, below, lower


def panel_rows(rows, first, upper, below, lower):
    position = first + iota((rows.shape[0], PIV), 0)
    left = jnp.where(position >= PIV, mm3(rows[:, 0:PIV], upper), 0.0)
    right = rows[:, PIV:KU] - mm3(left, below, NT)
    last = jnp.where(position >= KU, mm3(right, lower), 0.0)
    keep = jnp.concatenate(
        [jnp.where(position >= PIV, rows[:, 0:PIV], 0.0), jnp.where(position >= KU, right, 0.0)], axis=1
    )
    return jnp.concatenate([left, last], axis=1), keep


def mid_kernel(
    where, front, both, from_x, from_y, from_core, cross, left, cols, parts, send, rows
):
    low, high, pos = where[0], where[1], where[2]

    @pl.when(pos == 0)
    def _():
        rows[...] = both[0:HALF, :]

    @pl.when(pos == 2)
    def _():
        rows[...] = from_x[0:HALF, :]

    @pl.when(pos % 2 == 1)
    def _():
        rows[...] = from_core[0:HALF, :]

    own_cols = pl.multiple_of((pos % 2) * QUARTER, QUARTER)
    other_cols = jnp.where(
        pos == 0,
        from_y[0:QUARTER, :],
        jnp.where(pos == 1, from_core[HALF : HALF + QUARTER, :], cross[...]),
    )
    col_rows = jnp.where(pos // 2 == low, rows[pl.ds(own_cols, QUARTER), :], other_cols)
    other_pivots = jnp.where(pos == 1, from_core[HALF + QUARTER :, :], other_cols[0:KU, :])
    pivots = jnp.where(low == 0, rows[0:KU, :], other_pivots)
    upper, below, lower = panel_parts(
        pivots[0:PIV, 0:PIV], pivots[PIV:KU, 0:PIV], pivots[PIV:KU, PIV:KU]
    )
    parts[0], parts[1], parts[2] = upper, below, lower
    _, col_keep = panel_rows(col_rows, pos * QUARTER, upper, below, lower)
    cols[...] = col_keep
    start = pl.multiple_of((1 - high) * QUARTER, QUARTER)
    row_left, _ = panel_rows(
        rows[pl.ds(start, QUARTER), :], low * HALF + start, upper, below, lower
    )
    left[...] = row_left
    send[...] = front[pl.ds(start, QUARTER), :].astype(F32) - mm3(row_left, col_keep, NT)


def spread(values, places, other):
    row_place, col_place = places[2 * other], places[2 * other + 1]
    return pick_cols(pick_rows(row_place, values), col_place)


def own_kernel(
    where, front, both, from_x, from_core, left, cols, parts, places, factor, out, own
):
    low, high, pos = where[0], where[1], where[2]
    start = pl.multiple_of(high * QUARTER, QUARTER)
    here = pl.ds(start, QUARTER)
    rows = jnp.where(
        pos == 0, both[here, :], jnp.where(pos == 2, from_x[here, :], from_core[here, :])
    )
    row_left, _ = panel_rows(rows, low * HALF + start, parts[0], parts[1], parts[2])
    own[...] = row_left
    slab = factor.shape[0]
    first = pos * slab
    inner = pl.ds(pl.multiple_of(first % QUARTER, slab), slab)
    factor[...] = jnp.where(first // QUARTER == high, own[inner, :], left[inner, :])
    block = front[here, :].astype(F32) - mm3(row_left, cols[...], NT)
    out[...] = spread(block, places, 0)


def other_kernel(block, places, base, out):
    out[...] = base[...] + spread(block[...], places, 1)


def top_kernel(where, front, rows, here, first, from_y, from_core, base, out):
    low, pos, quarter = where[0], where[2], where[3]
    col_rows = jnp.where(low == pos // 2, here[...], from_y[...])
    pivots = jnp.where(
        low == 0, first[...], jnp.where(pos == 1, from_core[...], from_y[0:KU, :])
    )
    upper, below, lower = panel_parts(
        pivots[0:PIV, 0:PIV], pivots[PIV:KU, 0:PIV], pivots[PIV:KU, PIV:KU]
    )
    row_left, _ = panel_rows(rows[...], quarter * QUARTER, upper, below, lower)
    _, col_keep = panel_rows(col_rows, pos * QUARTER, upper, below, lower)
    out[...] = base[...] + front[...].astype(F32) - mm3(row_left, col_keep, NT)


def gather_kernel(count, where, *refs):
    sources, out = refs[0:count], refs[-1]
    row_first = where[3] * QUARTER
    col_first = where[2] * QUARTER
    units = [source.at[unit] for source in sources for unit in range(source.shape[0])]
    leaves, _, width = units[0].shape
    total = refs[count][...] if len(refs) > count + 1 else jnp.zeros(out.shape, F32)
    spots = iota((QUARTER, width), 0)
    for first in range(0, len(units), 2):
        row_places, blocks = [], []
        for unit in units[first : first + 2]:
            for leaf in range(leaves):
                link = unit[leaf, width : width + 1, :].astype(jnp.int32)
                row_places.append(onehot(spots == link - row_first))
                col_places = onehot(spots == link - col_first)
                blocks.append(pick_cols(unit[leaf, 0:width, :], col_places))
        total = total + pick_rows(
            jnp.concatenate(row_places, axis=1), jnp.concatenate(blocks, axis=0)
        )
    out[...] = total


def gather_kernel_of(count):
    return functools.partial(gather_kernel, count)


def stack_kernel(count, *refs):
    first = 0
    for part in refs[0:count]:
        refs[count][first : first + part.shape[0]] = part[...]
        first += part.shape[0]


def stack(parts, after):
    shape = (sum(part.shape[0] for part in parts),) + parts[0].shape[1:]
    return call(functools.partial(stack_kernel, len(parts)), [shape], parts, after, scalars=False)


def cast_kernel(mid_part, top_part, both, mid_cols):
    values = mid_part[...].astype(F32)
    mid_cols[...] = values
    both[0:HALF, :] = values
    both[HALF:, :] = top_part[...].astype(F32)


def relay_kernel(where, both, from_x, from_y, core, cross):
    here = where[2] == 0
    core[0:HALF, :] = jnp.where(here, both[0:HALF, :], from_x[0:HALF, :])
    core[HALF : HALF + QUARTER, :] = from_y[QUARTER:HALF, :]
    core[HALF + QUARTER :, :] = from_y[0:KU, :]
    far = jnp.where(where[0] == 0, from_y[QUARTER:HALF, :], from_y[0:QUARTER, :])
    cross[...] = jnp.where(here, far, from_x[0:QUARTER, :])


def choose_kernel(where, both, from_x, out):
    out[...] = jnp.where(where[2] == 0, both[HALF:, :], from_x[HALF:, :])


def pair_kernel(where, top_rows, top_z, pair):
    first = where[1] == 0
    pair[0:QUARTER, :] = jnp.where(first, top_rows[...], top_z[...])
    pair[QUARTER:, :] = jnp.where(first, top_z[...], top_rows[...])


def here_kernel(where, pair, from_core, rows, out, first):
    even = where[2] % 2 == 0
    own = pl.ds(pl.multiple_of(where[1] * QUARTER, QUARTER), QUARTER)
    rows[...] = jnp.where(even, pair[own, :], from_core[own, :])
    low_half = jnp.where(even, pair[0:QUARTER, :], from_core[0:QUARTER, :])
    first[...] = low_half[0:KU, :]
    second = jnp.logical_and(jnp.logical_not(even), where[2] // 2 == where[0])
    out[...] = jnp.where(second, from_core[QUARTER:, :], low_half)


def first_kernel(from_y, out):
    out[...] = from_y[0:KU, :]


COST = pl.CostEstimate(flops=10**9, bytes_accessed=1000, transcendentals=0)
FENCE = pl.CostEstimate(flops=3 * 10**10, bytes_accessed=1000, transcendentals=0)


def call(body, outs, args, after=(), scalars=True, scratch=(), fence=False, far=(), kind=F32):
    specs = [pl.BlockSpec(memory_space=pltpu.VMEM) for _ in args]
    if scalars:
        specs[0] = pl.BlockSpec(memory_space=pltpu.SMEM)
    for index in far:
        specs[index] = pl.BlockSpec(memory_space=pltpu.HBM)
    given = len(args)
    skipped = len(after)

    def kernel(*refs):
        body(*refs[:given], *refs[given + skipped :])

    shapes = [jax.ShapeDtypeStruct(shape, kind) for shape in outs]
    single = len(shapes) == 1
    return pl.pallas_call(
        kernel,
        out_shape=shapes[0] if single else shapes,
        in_specs=specs + [pl.BlockSpec(memory_space=pl.ANY) for _ in after],
        out_specs=(
            pl.BlockSpec(memory_space=pltpu.VMEM)
            if single
            else [pl.BlockSpec(memory_space=pltpu.VMEM) for _ in shapes]
        ),
        scratch_shapes=list(scratch),
        compiler_params=pltpu.CompilerParams(vmem_limit_bytes=24 * 2**20),
        cost_estimate=FENCE if fence else COST,
    )(*args, *after)


def local(
    kkt_blocks,
    kkt_owner,
    kkt_target,
    leaf_pivot,
    pivot_signs,
    perturb,
    leaf_coupling,
    leaf_map,
    mid_front,
    level_map,
    top_front,
):
    cube_count = lax.axis_size("cube")
    front_count = lax.axis_size("front")
    cube = lax.axis_index("cube")
    front = lax.axis_index("front")
    b0 = cube % 2
    b1 = cube // 2 % 2
    quarter = 2 * b0 + b1
    where = jnp.stack([b0, b1, front, quarter, cube // 2]).astype(jnp.int32)

    def move(array, rule):
        pairs = []
        for source_cube in range(cube_count):
            for source_front in range(front_count):
                target = rule(source_cube % 2, source_cube // 2 % 2, source_front)
                if target is not None:
                    new_cube = source_cube // 4 * 4 + 2 * target[1] + target[0]
                    pairs.append(
                        (source_cube * front_count + source_front, new_cube * front_count + target[2])
                    )
        return lax.ppermute(array, AXES, pairs)

    blocks = kkt_blocks[0]
    block_count, width = blocks.shape
    capacity = max(2, 2 * block_count // cube_count)
    slots = -(-(capacity + 1) // 8) * 8

    both, mid_cols = call(
        cast_kernel,
        [(HALF + QUARTER, KU), (HALF, KU)],
        [mid_front[:, 0:KU], top_front[:, 0:KU]],
        scalars=False,
    )
    both_x = move(both, lambda y, z, f: (y, z, 2) if f == 0 else None)
    mid_y = move(mid_cols, lambda y, z, f: (1 - y, z, 0) if f == 0 else None)

    packed, packed_token = call(
        functools.partial(pack_kernel, capacity, slots, cube_count),
        [(cube_count * slots, width), (8, width)],
        [blocks, kkt_owner.reshape(1, block_count), kkt_target.reshape(1, block_count)],
        [both],
        scalars=False,
    )
    got = lax.all_to_all(
        packed.reshape(cube_count, slots, width), "cube", split_axis=0, concat_axis=0, tiled=True
    )

    leaves = leaf_pivot.shape[0]
    size = leaf_pivot.shape[2]
    inverse, links, coupling = call(
        prepare_kernel,
        [(leaves, size, size), (8, size), leaf_coupling.shape],
        [where, leaf_pivot, leaf_coupling, pivot_signs, perturb, leaf_map, level_map],
        [packed_token],
        scratch=[pltpu.VMEM(leaf_pivot.shape, F32), pltpu.SemaphoreType.DMA((2,))],
        far=(1, 2),
    )
    places, places_token = call(
        places_kernel,
        [(4, QUARTER, QUARTER), (16, PIV)],
        [where, level_map],
        [links],
        kind=BF16,
    )

    to_core, to_cross = call(
        relay_kernel,
        [(HALF + QUARTER + KU, KU), (QUARTER, KU)],
        [where, both, both_x, mid_y],
        [places_token, got],
    )
    mid_cross = move(to_cross, lambda y, z, f: {0: (y, z, 3), 2: (1 - y, z, 2)}.get(f))
    mid_core = move(to_core, lambda y, z, f: (y, z, f + 1) if f % 2 == 0 else None)

    top_rows = call(choose_kernel, [(QUARTER, KU)], [where, both, both_x], [to_core])
    top_z = move(top_rows, lambda y, z, f: (y, 1 - z, f))

    factor, sent = call(
        functools.partial(leaf_kernel, capacity, slots, cube_count),
        [leaf_coupling.shape, (leaves, size + 8, size)],
        [got, inverse, links, coupling],
        [to_core],
        scalars=False,
    )
    sent = sent[None]
    k_z = move(sent, lambda y, z, f: (y, 1 - z, f))
    mid_left, mid_keep, mid_parts, mid_send = call(
        mid_kernel,
        [(QUARTER, KU), (QUARTER, KU), (3, PIV, PIV), (QUARTER, QUARTER)],
        [where, mid_front, both, both_x, mid_y, mid_core, mid_cross],
        [sent],
        scratch=[pltpu.VMEM((HALF, KU), F32)],
        fence=True,
    )
    mid_other = move(mid_send, lambda y, z, f: (y, 1 - z, f))

    square = [(QUARTER, QUARTER)]
    k_own = stack([sent, k_z], [mid_send])
    k_x = move(k_own, lambda y, z, f: (y, z, f ^ 2))
    k_y = move(k_own, lambda y, z, f: (1 - y, z, f))
    pair = call(pair_kernel, [(HALF, KU)], [where, top_rows, top_z], [k_own])
    pair_core = move(pair, lambda y, z, f: (y, z, f ^ 1))
    top_own, here, top_first = call(
        here_kernel,
        [(QUARTER, KU), (QUARTER, KU), (KU, KU)],
        [where, pair, pair_core],
    )
    top_y = move(here, lambda y, z, f: (1 - y, z, f))
    mid_factor, upper = call(
        own_kernel,
        [(HALF // front_count, KU), (QUARTER, QUARTER)],
        [where, mid_front, both, both_x, mid_core, mid_left, mid_keep, mid_parts, places],
        [here],
        scratch=[pltpu.VMEM((QUARTER, KU), F32)],
    )
    to_x = stack([k_y], [upper])
    k_xy = move(to_x, lambda y, z, f: (y, z, f ^ 2))
    units = stack([k_own, k_x, k_y], [to_x])
    swapped = move(units, lambda y, z, f: (y, z, f ^ 1))
    upper = call(gather_kernel_of(3), square, [where, k_own, k_x, k_y, upper], [units], fence=True)
    upper = call(gather_kernel_of(1), square, [where, swapped, upper])
    units = stack([k_xy], [upper])
    swapped = move(units, lambda y, z, f: (y, z, f ^ 1))
    upper = call(gather_kernel_of(1), square, [where, k_xy, upper], [units], fence=True)
    from_y = call(first_kernel, [(KU, KU)], [top_y], [upper], scalars=False)
    top_core = move(from_y, lambda y, z, f: (y, z, f ^ 1))
    upper = call(gather_kernel_of(1), square, [where, swapped, upper], [from_y])
    upper = call(
        top_kernel,
        square,
        [where, top_front, top_own, here, top_first, top_y, top_core, upper],
    )
    upper = call(other_kernel, square, [mid_other, places, upper], scalars=False)
    return factor, mid_factor, upper


def solution(mesh):
    in_specs = (
        P("front", "cube", None),
        P("front", "cube", None),
        P("front", "cube"),
        P("cube", "front", None),
        P("cube", "front"),
        P("cube", "front"),
        P("cube", "front", None),
        P("cube", "front"),
        P("cube", "front"),
        P(),
        P("cube", "front"),
    )
    out_specs = (P("cube", "front", None), P(("cube", "front"), None), P("cube", "front"))
    return jax.shard_map(local, mesh=mesh, in_specs=in_specs, out_specs=out_specs, check_vma=False)
```
